256 devices in a mesh: plane: 16 (over x, y), ax: 16 (over z, core).
Axes of the slice: x: 4, y: 4, z: 8, core: 2. Of those that a mesh axis runs over, the one named last changes fastest.
Arguments:
- source: float32 [1024, 256, 128], P('plane', 'ax'), may hold values from -6 to 6
- radial_basis: float32 [1024, 128, 128], P('plane'), may hold values from -0.5 to 0.5
- radial_weights: float32 [128], replicated, may hold values from 0.4 to 1.6
- mode_shifts: float32 [1024, 128], P('plane'), may hold values from 0.0001 to 0.03
Outputs:
- pressure: float32 [1024, 256, 128], P('plane', 'ax')
The draws below stay inside these ranges and needn't reach their ends.
All inputs are finite; a program needn't handle non-finite values.
Results may differ from the reference program's by a relative error of at most 0.0003.
Values sent between devices are 32-bit elements; how exact they have to be, the bound alone decides.
No kernel may reach another device: no remote copies, remote signals or barrier semaphores. Data moves between devices by JAX's collectives and lax.ppermute only.
A program may use at most 64 MiB of HBM per device.

```python
import math
import jax
import jax.numpy as jnp
from jax import lax

NT = 1024
NR = 128
NZ = 256


def block_scale(stream_key, dims, cuts, smallest, top_value):
    gain, own = 1.0, jax.random.fold_in(stream_key, 6)
    for position, shards_of in cuts:
        steps = jnp.exp(jax.random.uniform(jax.random.fold_in(own, position), (shards_of,), jnp.float32, smallest / len(cuts), top_value / len(cuts)))
        gain = gain * jnp.repeat(steps, dims[position] // shards_of).reshape([-1 if axis == position else 1 for axis in range(len(dims))])
    return gain


def centred(stream_key, shape, scale, limit, split=(), kind=jnp.bfloat16):
    values = scale * jax.random.normal(stream_key, shape, jnp.float32)
    if split:
        values = values * block_scale(stream_key, shape, split, -0.22, 0.18)
    return jnp.clip(values, -limit, limit).astype(kind)


def setup_inputs(seed: int = 0) -> dict:
    key_of = jax.random.split(jax.random.key(seed), 5)
    source = centred(key_of[0], (NT, NZ, NR), 1.0, 6.0, ((0, 16), (1, 16)), jnp.float32)
    radial_basis = centred(key_of[1], (NT, NR, NR), NR ** -0.5, 0.5, ((0, 16),), jnp.float32)
    radial_weights = jnp.clip(1.0 + 0.12 * jax.random.normal(key_of[2], (NR,), jnp.float32), 0.4, 1.6)
    mode_shifts = jnp.clip(jnp.exp(math.log(0.03) - 5.7037825 * jax.random.uniform(key_of[3], (NT, NR), jnp.float32) ** block_scale(key_of[3], (NT, NR), ((0, 16),), -0.2, 0.2)), 0.0001, 0.03)
    return dict(source=source, radial_basis=radial_basis, radial_weights=radial_weights, mode_shifts=mode_shifts)


axial_scale = 0.01

def basis_entry(mode_grid, angle_grid, length):
    middle = length // 2
    harmonic = jnp.where(mode_grid <= middle, mode_grid, mode_grid - middle)
    wrapped = harmonic * angle_grid % length
    radians = wrapped.astype(jnp.float32) * (2.0 * math.pi / length)
    factor = jnp.where((mode_grid == 0) | (mode_grid == middle), math.sqrt(1.0 / length), math.sqrt(2.0 / length))
    return jnp.where(mode_grid <= middle, jnp.cos(radians), jnp.sin(radians)) * factor

def tridiagonal_sweep(diagonal, rights):

    def forward(running, current):
        prior_factor, prior_carried = running
        denominator = diagonal + prior_factor
        multiplier = -1.0 / denominator
        carried = (current + prior_carried) / denominator
        return ((multiplier, carried), (multiplier, carried))
    zeroed = jnp.zeros_like(rights[0])
    finished, (factors, carries) = lax.scan(forward, (zeroed, zeroed), rights)

    def backward(following, entries):
        multiplier, carried = entries
        result = carried - multiplier * following
        return (result, result)
    finished, solved = lax.scan(backward, zeroed, (factors, carries), reverse=True)
    return solved

def reference(source, radial_basis, radial_weights, mode_shifts):
    harmonics = jnp.arange(NT, dtype=jnp.int32)
    fourier = basis_entry(harmonics[:, None], harmonics[None, :], NT)
    spectral = jnp.dot(fourier, source.reshape(NT, NZ * NR), precision=lax.Precision.HIGHEST, preferred_element_type=jnp.float32).reshape(NT, NZ, NR)
    spectra = jnp.einsum('kzr,krj->zkj', spectral * radial_weights, radial_basis, precision=lax.Precision.HIGHEST)
    solved = tridiagonal_sweep(2.0 + mode_shifts, spectra * axial_scale)
    radial_field = jnp.einsum('zkj,krj->kzr', solved, radial_basis, precision=lax.Precision.HIGHEST)
    return jnp.dot(fourier.T, radial_field.reshape(NT, NZ * NR), precision=lax.Precision.HIGHEST, preferred_element_type=jnp.float32).reshape(NT, NZ, NR)
```

```python
import functools
import math

import jax
import jax.numpy as jnp
import ml_dtypes
import numpy as np
from jax import lax
from jax.experimental import pallas as pl
from jax.experimental.pallas import tpu as pltpu
from jax.sharding import PartitionSpec as P

axial_scale = 0.01
merge = 2
bf16 = jnp.bfloat16
f32 = jnp.float32


def mode_order(total, planes, share):
    local = total // planes
    size = local // share
    share_at, plane_at, parity, half = np.meshgrid(
        np.arange(share), np.arange(planes), np.arange(2), np.arange(size // 2), indexing="ij"
    )
    return plane_at * local + share_at * size + 2 * half + parity


def fourier_halves(total, planes, share):
    order = mode_order(total, planes, share).transpose(2, 0, 1, 3).reshape(2, total // 2)
    angles = np.arange(total // 2)
    middle = total // 2
    harmonic = np.where(order <= middle, order, order - middle)
    radians = (harmonic[:, :, None] * angles % total) * (2.0 * math.pi / total)
    factor = np.where((order == 0) | (order == middle), math.sqrt(1.0 / total), math.sqrt(2.0 / total))
    waves = np.where((order <= middle)[:, :, None], np.cos(radians), np.sin(radians))
    return (waves * factor[:, :, None]).astype(np.float32)


def split_table(table, parts):
    rest = table.astype(np.float32)
    pieces = []
    for _ in range(parts):
        piece = rest.astype(ml_dtypes.bfloat16)
        pieces.append(piece)
        rest = rest - piece.astype(np.float32)
    return np.stack(pieces)


def split2(value):
    high = value.astype(bf16)
    return high, (value - high.astype(f32)).astype(bf16)


def split3(value):
    high = value.astype(bf16)
    rest = value - high.astype(f32)
    middle = rest.astype(bf16)
    return high, middle, (rest - middle.astype(f32)).astype(bf16)


def mul(left, right):
    return jnp.dot(left, right, preferred_element_type=f32)


def mul_t(left, right):
    return lax.dot_general(left, right, (((1,), (1,)), ((), ())), preferred_element_type=f32)


def forward_kernel(table_ref, x_ref, out_ref):
    half_t = x_ref.shape[0] // 2
    width = x_ref.shape[1]
    blocks, size, _ = out_ref.shape
    low, high = x_ref[:half_t], x_ref[half_t:]
    for parity in range(2):
        folded = low + high if parity == 0 else low - high
        a, b, c = split3(folded)
        pair = jnp.concatenate([a, b], axis=1)
        first = mul(table_ref[0, parity], pair)
        second = mul(table_ref[1, parity], pair)
        third = mul(table_ref[0, parity], c) + mul(table_ref[2, parity], a)
        result = first[:, :width] + (
            (first[:, width:] + second[:, :width]) + (third + second[:, width:])
        )
        out_ref[:, parity * (size // 2) : (parity + 1) * (size // 2), :] = result.reshape(
            blocks, size // 2, width
        )


def backward_kernel(table_ref, x_ref, out_ref):
    blocks, size, width = x_ref.shape
    sums = []
    for parity in range(2):
        part = x_ref[:, parity * (size // 2) : (parity + 1) * (size // 2), :].reshape(-1, width)
        a, b = split2(part)
        pair = jnp.concatenate([a, b], axis=1)
        first = mul(table_ref[0, parity], pair)
        sums.append(first[:, :width] + (first[:, width:] + mul(table_ref[1, parity], a)))
    half_t = out_ref.shape[0] // 2
    out_ref[:half_t] = sums[0] + sums[1]
    out_ref[half_t:] = sums[0] - sums[1]


def modal_kernel(x_ref, basis_ref, weights_ref, decay_ref, f_ref, carry_ref):
    depth, size, _ = x_ref.shape
    weights = weights_ref[...]
    for place in range(size):
        parity, half = divmod(place, size // 2)
        a, b, c = split3(x_ref[:, place, :] * weights)
        ra, rb, rc = split3(basis_ref[2 * half + parity])
        small = mul(a, rc) + mul(c, ra) + mul(b, rb)
        f_ref[:, place, :] = mul(a, ra) + ((mul(a, rb) + mul(b, ra)) + small)
    decay = decay_ref[...]
    up = f_ref[0]
    down = f_ref[depth - 1]
    for step in range(1, depth):
        up = up * decay + f_ref[step]
        down = down * decay + f_ref[depth - 1 - step]
    carry_ref[0] = up
    carry_ref[1] = down


def solve_kernel(f_ref, basis_ref, decay_ref, gain_ref, start_ref, out_ref, y_ref):
    depth, size, _ = f_ref.shape
    decay = decay_ref[...]
    gain = gain_ref[...]
    up = start_ref[0]
    for step in range(depth):
        up = up * decay
        y_ref[step] = up
        up = up + f_ref[step]
    down = start_ref[1]
    for step in range(depth - 1, -1, -1):
        down = down * decay + f_ref[step]
        y_ref[step] = (y_ref[step] + down) * gain
    for place in range(size):
        parity, half = divmod(place, size // 2)
        a, b = split2(y_ref[:, place, :])
        ra, rb = split2(basis_ref[2 * half + parity])
        out_ref[:, place, :] = mul_t(a, ra) + (mul_t(a, rb) + mul_t(b, ra))


def whole(memory_space=pltpu.VMEM):
    return pl.BlockSpec(memory_space=memory_space)


def body(source, radial_basis, radial_weights, mode_shifts):
    planes = lax.axis_size("plane")
    blocks = lax.axis_size("ax")
    local_t, depth_cells, radius_count = source.shape
    total_t = local_t * planes
    axial_cells = depth_cells * blocks
    size = local_t // merge
    span = depth_cells * merge
    table = fourier_halves(total_t, planes, merge)
    forward_table = jnp.asarray(split_table(table, 3))
    backward_table = jnp.asarray(split_table(table.transpose(0, 2, 1), 2))
    teams = [
        [plane * blocks + first + share for share in range(merge) for plane in range(planes)]
        for first in range(0, blocks, merge)
    ]

    axial_index = lax.axis_index("ax")
    share = axial_index % merge
    block = axial_index // merge
    shifts = lax.dynamic_slice_in_dim(mode_shifts, share * size, size, 0)
    shifts = shifts.reshape(size // 2, 2, radius_count).transpose(1, 0, 2).reshape(size, radius_count)
    basis = lax.dynamic_slice_in_dim(radial_basis, share * size, size, 0)
    rounded = lax.reduce_precision(2.0 + shifts, 8, 23) - 2.0
    rise = 0.5 * jnp.sqrt(rounded)
    cosh_half = jnp.sqrt(1.0 + rise * rise)
    root = cosh_half - rise
    decay = root * root
    gain = axial_scale / (4.0 * rise * cosh_half)

    def power(base, count):
        result = None
        while count:
            if count & 1:
                result = base if result is None else result * base
            base = base * base
            count >>= 1
        return result

    def device_power(base, count, limit):
        result = jnp.ones_like(base)
        bit = 1
        while bit < limit:
            result = jnp.where((count & bit) != 0, result * base, result)
            base = base * base
            bit *= 2
        return result

    teams_along = blocks // merge
    span_decay = power(decay, span)
    to_first = device_power(span_decay, block, teams_along)
    to_last = device_power(span_decay, teams_along - 1 - block, teams_along)
    whole_decay = power(decay, axial_cells + 1)
    closing = decay / (1.0 - whole_decay * whole_decay)

    piece = lax.all_to_all(source.transpose(1, 0, 2), "plane", 0, 0, tiled=True)
    spectral = pl.pallas_call(
        forward_kernel,
        out_shape=jax.ShapeDtypeStruct((planes * merge, size, radius_count), f32),
        in_specs=[whole(), whole()],
        out_specs=whole(),
        name="fourier_forward",
    )(forward_table, piece.reshape(total_t, radius_count))
    modal = lax.all_to_all(
        spectral, ("plane", "ax"), 0, 0, tiled=True, axis_index_groups=teams
    )
    spectra, carries = pl.pallas_call(
        modal_kernel,
        out_shape=(
            jax.ShapeDtypeStruct((span, size, radius_count), f32),
            jax.ShapeDtypeStruct((2, size, radius_count), f32),
        ),
        in_specs=[whole()] * 4,
        out_specs=(whole(), whole()),
        name="radial_forward",
    )(modal, basis, radial_weights.reshape(1, radius_count), decay)

    up, down = carries[0], carries[1]
    from_below = jnp.zeros_like(up)
    from_above = jnp.zeros_like(up)
    reach = 1
    reach_decay = span_decay
    while reach < teams_along:
        stride = reach * merge
        swap = [(index, index ^ stride) for index in range(blocks)]
        other = lax.ppermute(jnp.stack([up, down]), "ax", swap)
        above = (block & reach) != 0
        offset = block & (reach - 1)
        near_below = device_power(span_decay, offset, reach)
        near_above = device_power(span_decay, reach - 1 - offset, reach)
        from_below = jnp.where(above, from_below + near_below * other[0], from_below)
        from_above = jnp.where(above, from_above, from_above + near_above * other[1])
        up = jnp.where(above, up + reach_decay * other[0], other[0] + reach_decay * up)
        down = jnp.where(above, other[1] + reach_decay * down, down + reach_decay * other[1])
        reach *= 2
        reach_decay = reach_decay * reach_decay
    start_below = from_below - closing * (down - whole_decay * up) * to_first
    start_above = from_above - closing * (up - whole_decay * down) * to_last

    radial_field = pl.pallas_call(
        solve_kernel,
        out_shape=jax.ShapeDtypeStruct((span, size, radius_count), f32),
        in_specs=[whole()] * 5,
        out_specs=whole(),
        scratch_shapes=[pltpu.VMEM((span, size, radius_count), f32)],
        name="solve_and_radial_back",
    )(spectra, basis, decay, gain, jnp.stack([start_below, start_above]))
    collected = lax.all_to_all(
        radial_field, ("plane", "ax"), 0, 0, tiled=True, axis_index_groups=teams
    )
    spatial = pl.pallas_call(
        backward_kernel,
        out_shape=jax.ShapeDtypeStruct((total_t, radius_count), f32),
        in_specs=[whole(), whole()],
        out_specs=whole(),
        name="fourier_backward",
    )(backward_table, collected)
    pressure = lax.all_to_all(
        spatial.reshape(planes, local_t, radius_count), "plane", 0, 0, tiled=True
    )
    return pressure.transpose(1, 0, 2)


def solution(mesh):
    placed = (P("plane", "ax", None), P("plane", None, None), P(), P("plane", None))
    return jax.shard_map(
        body, mesh=mesh, in_specs=placed, out_specs=P("plane", "ax", None), check_vma=False
    )
```

```python
import functools
import math

import jax
import jax.numpy as jnp
import ml_dtypes
import numpy as np
from jax import lax
from jax.experimental import pallas as pl
from jax.experimental.pallas import tpu as pltpu
from jax.sharding import PartitionSpec as P

axial_scale = 0.01
merge = 4
bf16 = jnp.bfloat16
f32 = jnp.float32
compact = pltpu.CompilerParams(vmem_limit_bytes=16 * 2**20)


def mode_order(total, planes, share):
    local = total // planes
    size = local // share
    share_at, plane_at, parity, half = np.meshgrid(
        np.arange(share), np.arange(planes), np.arange(2), np.arange(size // 2), indexing="ij"
    )
    return plane_at * local + share_at * size + 2 * half + parity


def fourier_halves(total, planes, share):
    order = mode_order(total, planes, share).transpose(2, 0, 1, 3).reshape(2, total // 2)
    angles = np.arange(total // 2)
    middle = total // 2
    harmonic = np.where(order <= middle, order, order - middle)
    radians = (harmonic[:, :, None] * angles % total) * (2.0 * math.pi / total)
    factor = np.where((order == 0) | (order == middle), math.sqrt(1.0 / total), math.sqrt(2.0 / total))
    waves = np.where((order <= middle)[:, :, None], np.cos(radians), np.sin(radians))
    return (waves * factor[:, :, None]).astype(np.float32)


def split_table(table):
    high = table.astype(ml_dtypes.bfloat16)
    rest = (table - high.astype(np.float32)).astype(ml_dtypes.bfloat16)
    return np.concatenate([high, rest], axis=2)


def split2(value):
    high = value.astype(bf16)
    return high, (value - high.astype(f32)).astype(bf16)


def split3(value):
    high = value.astype(bf16)
    rest = value - high.astype(f32)
    middle = rest.astype(bf16)
    return high, middle, (rest - middle.astype(f32)).astype(bf16)


def mul(left, right):
    return jnp.dot(left, right, preferred_element_type=f32)


def mul_t(left, right):
    return lax.dot_general(left, right, (((1,), (1,)), ((), ())), preferred_element_type=f32)


def twice(value, axis):
    return jnp.concatenate([value, value], axis=axis)


def swaps(teams):
    rounds = []
    reach = 1
    while reach < teams:
        if 2 * reach == teams and teams == 4:
            rounds.append([team ^ 3 for team in range(teams)])
        elif 2 * reach == teams and teams >= 8:
            wide = teams // 8
            far = (6, 7, 4, 5, 2, 3, 0, 1)
            rounds.append([far[team // wide] * wide + team % wide for team in range(teams)])
        else:
            rounds.append([team ^ reach for team in range(teams)])
        reach *= 2
    return rounds


def prepare_kernel(
    source_ref, shifts_ref, table_ref, out_ref, hold_ref, decay_ref, gain_ref, mix_ref, near_ref, end_ref,
    held_ref, shift_ref, sems, extra_sems,
):
    cells, angles, _ = out_ref.shape
    size = decay_ref.shape[0]
    rounds = near_ref.shape[0]
    teams = 2**rounds
    chunks = sems.shape[0]
    rows = angles // chunks
    shift_copy = pltpu.make_async_copy(shifts_ref, shift_ref, extra_sems.at[0])
    table_copy = pltpu.make_async_copy(table_ref, hold_ref, extra_sems.at[1])
    copies = [
        pltpu.make_async_copy(
            source_ref.at[pl.ds(chunk * rows, rows)], held_ref.at[pl.ds(chunk * rows, rows)], sems.at[chunk]
        )
        for chunk in range(chunks)
    ]
    shift_copy.start()
    for copy in copies:
        copy.start()
    table_copy.start()

    position = lax.axis_index("ax")
    block = lax.div(position, jnp.int32(merge))
    first = lax.rem(position, jnp.int32(merge)) * size
    shift_copy.wait()
    shifts = jnp.concatenate(
        [shift_ref[pl.ds(first + parity, size // 2, stride=2), :] for parity in range(2)], axis=0
    )
    rise = 0.5 * jnp.sqrt((2.0 + shifts) - 2.0)
    cosh_half = jnp.sqrt(1.0 + rise * rise)
    root = cosh_half - rise
    decay = root * root
    decay_ref[...] = decay
    gain_ref[...] = axial_scale / (4.0 * rise * cosh_half)
    one = jnp.ones_like(decay)
    zero = jnp.zeros_like(decay)
    powers = [power(decay, cells * merge)]
    for _ in range(rounds):
        powers.append(powers[-1] * powers[-1])
    whole_decay = powers[-1] * decay

    def step_power(count, bits):
        result = one
        for bit in range(bits):
            result = jnp.where((count & (1 << bit)) != 0, result * powers[bit], result)
        return result

    for turn in range(rounds):
        reach = 1 << turn
        above = (block & reach) != 0
        offset = block & (reach - 1)
        mine = jnp.where(above, one, powers[turn])
        theirs = jnp.where(above, powers[turn], one)
        mix_ref[turn, 0, 0] = mine
        mix_ref[turn, 0, 1] = theirs
        mix_ref[turn, 1, 0] = theirs
        mix_ref[turn, 1, 1] = mine
        near_ref[turn, 0] = jnp.where(above, step_power(offset, turn), zero)
        near_ref[turn, 1] = jnp.where(above, zero, step_power(reach - 1 - offset, turn))
    closing = decay / (1.0 - whole_decay * whole_decay)
    to_first = closing * step_power(block, rounds)
    to_last = closing * step_power(teams - 1 - block, rounds)
    end_ref[0, 0] = to_first * whole_decay
    end_ref[0, 1] = -to_first
    end_ref[1, 0] = -to_last
    end_ref[1, 1] = to_last * whole_decay

    for chunk, copy in enumerate(copies):
        copy.wait()
        part = pl.ds(chunk * rows, rows)
        for cell in range(cells):
            out_ref[cell, part, :] = held_ref[part, cell, :]
    table_copy.wait()


def power(base, count):
    result = None
    while count:
        if count & 1:
            result = base if result is None else result * base
        base = base * base
        count >>= 1
    return result


def forward_kernel(table_ref, x_ref, out_ref):
    half_t = x_ref.shape[0] // 2
    width = x_ref.shape[1]
    blocks, size, _ = out_ref.shape
    low, high = x_ref[:half_t], x_ref[half_t:]
    for parity in range(2):
        folded = low + high if parity == 0 else low - high
        a, b, c = split3(folded)
        first = mul(table_ref[parity], twice(jnp.concatenate([a, b], axis=1), 0))
        result = first[:, :width] + (first[:, width:] + mul(table_ref[parity, :, :half_t], c))
        out_ref[:, parity * (size // 2) : (parity + 1) * (size // 2), :] = result.reshape(
            blocks, size // 2, width
        )


def backward_kernel(table_ref, x_ref, out_ref):
    blocks, size, width = x_ref.shape
    half_k = blocks * size // 2
    sums = []
    for parity in range(2):
        part = x_ref[:, parity * (size // 2) : (parity + 1) * (size // 2), :].reshape(-1, width)
        a, b = split2(part)
        first = mul(table_ref[parity, :, :half_k], jnp.concatenate([a, b], axis=1))
        sums.append(first[:, :width] + (first[:, width:] + mul(table_ref[parity, :, half_k:], a)))
    half_t = out_ref.shape[0] // 2
    out_ref[:half_t] = sums[0] + sums[1]
    out_ref[half_t:] = sums[0] - sums[1]


def first_mode(size):
    return lax.rem(lax.axis_index("ax"), jnp.int32(merge)) * size


def modal_kernel(x_ref, basis_ref, weights_ref, decay_ref, f_ref, carry_ref):
    depth, size, _ = x_ref.shape
    weights = weights_ref[...]
    first = first_mode(size)
    for place in range(size):
        parity, half = divmod(place, size // 2)
        values = jnp.concatenate(split3(x_ref[:, place, :] * weights), axis=0)
        basis = jnp.concatenate(split2(basis_ref[first + (2 * half + parity)]), axis=0)
        result = mul(twice(values, 1), basis)
        f_ref[:, place, :] = result[:depth] + (result[depth : 2 * depth] + result[2 * depth :])
    decay = decay_ref[...]
    up = f_ref[0]
    down = f_ref[depth - 1]
    for step in range(1, depth):
        up = up * decay + f_ref[step]
        down = down * decay + f_ref[depth - 1 - step]
    carry_ref[0] = up
    carry_ref[1] = down


def solve_kernel(f_ref, basis_ref, decay_ref, gain_ref, mix_ref, near_ref, end_ref, carry_ref, *refs):
    *other_refs, out_ref, up_ref, down_ref = refs
    depth, size, _ = f_ref.shape
    decay = decay_ref[...]
    first = first_mode(size)
    total = [carry_ref[0], carry_ref[1]]
    start = [jnp.zeros_like(decay)] * 2
    for turn, other_ref in enumerate(other_refs):
        other = [other_ref[0], other_ref[1]]
        start = [start[end] + near_ref[turn, end] * other[end] for end in range(2)]
        total = [mix_ref[turn, 0, end] * total[end] + mix_ref[turn, 1, end] * other[end] for end in range(2)]
    up, down = (start[end] + (end_ref[end, 0] * total[0] + end_ref[end, 1] * total[1]) for end in range(2))
    for step in range(depth):
        up = up * decay
        up_ref[step] = up
        up = up + f_ref[step]
        down = down * decay + f_ref[depth - 1 - step]
        down_ref[depth - 1 - step] = down
    for place in range(size):
        parity, half = divmod(place, size // 2)
        field = (up_ref[:, place, :] + down_ref[:, place, :]) * gain_ref[place : place + 1, :]
        values = jnp.concatenate(split2(field), axis=0)
        basis = jnp.concatenate(split2(basis_ref[first + (2 * half + parity)]), axis=1)
        result = mul_t(twice(values, 1), basis)
        out_ref[:, place, :] = result[:depth] + result[depth:]


def scatter_kernel(x_ref, out_ref, row_sems):
    rows = [
        pltpu.make_async_copy(x_ref.at[cell], out_ref.at[:, cell], row_sems.at[cell])
        for cell in range(x_ref.shape[0])
    ]
    for copy in rows:
        copy.start()
    for copy in rows:
        copy.wait()


def whole(memory_space=pltpu.VMEM):
    return pl.BlockSpec(memory_space=memory_space)


def in_vmem(value):
    return pltpu.with_memory_space_constraint(value, pltpu.VMEM)


def in_hbm(value):
    return pltpu.with_memory_space_constraint(value, pltpu.HBM)


def body(source, radial_basis, radial_weights, mode_shifts):
    planes = lax.axis_size("plane")
    blocks = lax.axis_size("ax")
    local_t, depth_cells, radius_count = source.shape
    total_t = local_t * planes
    size = local_t // merge
    span = depth_cells * merge
    teams = blocks // merge
    table = fourier_halves(total_t, planes, merge)
    forward_table = jnp.asarray(split_table(table))
    backward_table = jnp.asarray(split_table(table.transpose(0, 2, 1)))
    neighbours = [
        [plane * blocks + first + share for share in range(merge) for plane in range(planes)]
        for first in range(0, blocks, merge)
    ]
    rounds = swaps(teams)

    turned, held_table, decay, gain, mix, near, ends = pl.pallas_call(
        prepare_kernel,
        out_shape=(
            pltpu.VMEM((depth_cells, local_t, radius_count), f32),
            pltpu.VMEM(forward_table.shape, bf16),
            pltpu.VMEM((size, radius_count), f32),
            pltpu.VMEM((size, radius_count), f32),
            pltpu.VMEM((len(rounds), 2, 2, size, radius_count), f32),
            pltpu.VMEM((len(rounds), 2, size, radius_count), f32),
            pltpu.VMEM((2, 2, size, radius_count), f32),
        ),
        in_specs=[whole(pltpu.HBM)] * 3,
        out_specs=(whole(),) * 7,
        scratch_shapes=[
            pltpu.VMEM(source.shape, f32),
            pltpu.VMEM(mode_shifts.shape, f32),
            pltpu.SemaphoreType.DMA((4,)),
            pltpu.SemaphoreType.DMA((2,)),
        ],
        name="cells_first",
        compiler_params=compact,
    )(in_hbm(source), in_hbm(mode_shifts), in_hbm(forward_table))
    piece = lax.all_to_all(turned, "plane", 0, 0, tiled=True)
    spectral = pl.pallas_call(
        forward_kernel,
        out_shape=pltpu.VMEM((planes * merge, size, radius_count), f32),
        in_specs=[whole()] * 2,
        out_specs=whole(),
        name="fourier_forward",
        compiler_params=compact,
    )(in_vmem(held_table), in_vmem(piece.reshape(total_t, radius_count)))
    modal = lax.all_to_all(
        spectral, ("plane", "ax"), 0, 0, tiled=True, axis_index_groups=neighbours
    )
    spectra, carries = pl.pallas_call(
        modal_kernel,
        out_shape=(
            pltpu.VMEM((span, size, radius_count), f32),
            pltpu.VMEM((2, size, radius_count), f32),
        ),
        in_specs=[whole()] * 4,
        out_specs=(whole(), whole()),
        name="radial_forward",
        compiler_params=compact,
    )(in_vmem(modal), in_vmem(radial_basis), radial_weights.reshape(1, radius_count), in_vmem(decay))
    others = []
    sent = carries
    for turn, partners in enumerate(rounds):
        if turn:
            sent = mix[turn - 1, 0] * sent + mix[turn - 1, 1] * others[-1]
        pairs = [
            (team * merge + share, partner * merge + share)
            for team, partner in enumerate(partners)
            for share in range(merge)
        ]
        others.append(lax.ppermute(sent, "ax", pairs))
    radial_field = pl.pallas_call(
        solve_kernel,
        out_shape=pltpu.VMEM((span, size, radius_count), f32),
        in_specs=[whole()] * (8 + len(rounds)),
        out_specs=whole(),
        scratch_shapes=[pltpu.VMEM((span, size, radius_count), f32)] * 2,
        name="solve_and_radial_back",
        compiler_params=compact,
    )(
        in_vmem(spectra),
        in_vmem(radial_basis),
        in_vmem(decay),
        in_vmem(gain),
        in_vmem(mix),
        in_vmem(near),
        in_vmem(ends),
        in_vmem(carries),
        *map(in_vmem, others),
    )
    collected = lax.all_to_all(
        radial_field, ("plane", "ax"), 0, 0, tiled=True, axis_index_groups=neighbours
    )
    spatial = pl.pallas_call(
        backward_kernel,
        out_shape=pltpu.VMEM((total_t, radius_count), f32),
        in_specs=[whole()] * 2,
        out_specs=whole(),
        name="fourier_backward",
        compiler_params=compact,
    )(in_vmem(backward_table), in_vmem(collected))
    pressure = lax.all_to_all(
        spatial.reshape(planes, local_t, radius_count), "plane", 0, 0, tiled=True
    )
    return pl.pallas_call(
        scatter_kernel,
        out_shape=jax.ShapeDtypeStruct(source.shape, f32),
        in_specs=[whole()],
        out_specs=whole(pltpu.HBM),
        scratch_shapes=[pltpu.SemaphoreType.DMA((depth_cells,))],
        name="angles_first",
        compiler_params=compact,
    )(in_vmem(pressure))


def solution(mesh):
    placed = (P("plane", "ax", None), P("plane", None, None), P(), P("plane", None))
    return jax.shard_map(
        body, mesh=mesh, in_specs=placed, out_specs=P("plane", "ax", None), check_vma=False
    )
```

```python
import functools
import math

import jax
import jax.numpy as jnp
import ml_dtypes
import numpy as np
from jax import lax
from jax.experimental import pallas as pl
from jax.experimental.pallas import tpu as pltpu
from jax.sharding import PartitionSpec as P

axial_scale = 0.01
cores = 2
merge = 2
bf16 = jnp.bfloat16
f32 = jnp.float32
compact = pltpu.CompilerParams(vmem_limit_bytes=16 * 2**20)


def mode_order(total, planes, share):
    local = total // planes
    size = local // share
    share_at, plane_at, parity, half = np.meshgrid(
        np.arange(share), np.arange(planes), np.arange(2), np.arange(size // 2), indexing="ij"
    )
    return plane_at * local + share_at * size + 2 * half + parity


def fourier_halves(total, planes, share):
    order = mode_order(total, planes, share).transpose(2, 0, 1, 3).reshape(2, total // 2)
    angles = np.arange(total // 2)
    middle = total // 2
    harmonic = np.where(order <= middle, order, order - middle)
    radians = (harmonic[:, :, None] * angles % total) * (2.0 * math.pi / total)
    factor = np.where((order == 0) | (order == middle), math.sqrt(1.0 / total), math.sqrt(2.0 / total))
    waves = np.where((order <= middle)[:, :, None], np.cos(radians), np.sin(radians))
    return (waves * factor[:, :, None]).astype(np.float32)


def split_table(table):
    high = table.astype(ml_dtypes.bfloat16)
    rest = (table - high.astype(np.float32)).astype(ml_dtypes.bfloat16)
    return np.concatenate([high, rest], axis=2)


def split2(value):
    high = value.astype(bf16)
    return high, (value - high.astype(f32)).astype(bf16)


def split3(value):
    high = value.astype(bf16)
    rest = value - high.astype(f32)
    middle = rest.astype(bf16)
    return high, middle, (rest - middle.astype(f32)).astype(bf16)


def mul(left, right):
    return jnp.dot(left, right, preferred_element_type=f32)


def mul_t(left, right):
    return lax.dot_general(left, right, (((1,), (1,)), ((), ())), preferred_element_type=f32)


def twice(value, axis):
    return jnp.concatenate([value, value], axis=axis)


def swaps(teams):
    rounds = []
    reach = 1
    while reach < teams:
        if 2 * reach == teams and teams == 4:
            rounds.append([team ^ 3 for team in range(teams)])
        elif 2 * reach == teams and teams >= 8:
            wide = teams // 8
            far = (6, 7, 4, 5, 2, 3, 0, 1)
            rounds.append([far[team // wide] * wide + team % wide for team in range(teams)])
        else:
            rounds.append([team ^ reach for team in range(teams)])
        reach *= 2
    return rounds


def prepare_kernel(
    source_ref, shifts_ref, table_ref, out_ref, hold_ref, decay_ref, gain_ref, link_ref, lead_ref, mix_ref, near_ref, end_ref,
    held_ref, shift_ref, sems, extra_sems,
):
    cells, angles, _ = out_ref.shape
    size = decay_ref.shape[0]
    rounds = near_ref.shape[0]
    teams = 2**rounds
    chunks = sems.shape[0]
    rows = angles // chunks
    shift_copy = pltpu.make_async_copy(shifts_ref, shift_ref, extra_sems.at[0])
    table_copy = pltpu.make_async_copy(table_ref, hold_ref, extra_sems.at[1])
    copies = [
        pltpu.make_async_copy(
            source_ref.at[pl.ds(chunk * rows, rows)], held_ref.at[pl.ds(chunk * rows, rows)], sems.at[chunk]
        )
        for chunk in range(chunks)
    ]
    shift_copy.start()
    for copy in copies:
        copy.start()
    table_copy.start()

    core, share, team = place_in_team()
    first = share * size
    shift_copy.wait()
    shifts = jnp.concatenate(
        [shift_ref[pl.ds(first + parity, size // 2, stride=2), :] for parity in range(2)], axis=0
    )
    rise = 0.5 * jnp.sqrt((2.0 + shifts) - 2.0)
    cosh_half = jnp.sqrt(1.0 + rise * rise)
    root = cosh_half - rise
    decay = root * root
    decay_ref[...] = decay
    gain_ref[...] = axial_scale / (4.0 * rise * cosh_half)
    one = jnp.ones_like(decay)
    zero = jnp.zeros_like(decay)

    inner = [one, power(decay, cells)]
    for _ in range(2):
        inner.append(inner[-1] * inner[1])
    on_first = core == 0

    def apart(distance):
        below = inner[-distance - 1] if distance < 0 else zero
        above = inner[distance - 1] if distance > 0 else zero
        return below, above

    for source in range(merge):
        for target in range(merge):
            gap = 2 * (source - target)
            for end in range(2):
                link_ref[0, target, source, end] = apart(gap)[end]
                link_ref[1, target, source, end] = jnp.where(
                    on_first, apart(gap + 1)[end], apart(gap - 1)[end]
                )
        early, late = 2 * source, 2 * source + 1
        for owner in range(2):
            near, far = (early, late) if owner == 0 else (late, early)
            link_ref[owner, merge, source, 0] = jnp.where(on_first, inner[3 - near], inner[3 - far])
            link_ref[owner, merge, source, 1] = jnp.where(on_first, inner[near], inner[far])
        lead_ref[source, 0] = jnp.where(on_first, inner[early], inner[late])
        lead_ref[source, 1] = jnp.where(on_first, inner[3 - early], inner[3 - late])

    powers = [inner[3] * inner[1]]
    for _ in range(rounds):
        powers.append(powers[-1] * powers[-1])
    whole_decay = powers[-1] * decay

    def step_power(count, bits):
        result = one
        for bit in range(bits):
            result = jnp.where((count & (1 << bit)) != 0, result * powers[bit], result)
        return result

    for turn in range(rounds):
        reach = 1 << turn
        above = (team & reach) != 0
        offset = team & (reach - 1)
        mine = jnp.where(above, one, powers[turn])
        theirs = jnp.where(above, powers[turn], one)
        mix_ref[turn, 0, 0] = mine
        mix_ref[turn, 0, 1] = theirs
        mix_ref[turn, 1, 0] = theirs
        mix_ref[turn, 1, 1] = mine
        near_ref[turn, 0] = jnp.where(above, step_power(offset, turn), zero)
        near_ref[turn, 1] = jnp.where(above, zero, step_power(reach - 1 - offset, turn))
    closing = decay / (1.0 - whole_decay * whole_decay)
    to_first = closing * step_power(team, rounds)
    to_last = closing * step_power(teams - 1 - team, rounds)
    end_ref[0, 0] = to_first * whole_decay
    end_ref[0, 1] = -to_first
    end_ref[1, 0] = -to_last
    end_ref[1, 1] = to_last * whole_decay

    for chunk, copy in enumerate(copies):
        copy.wait()
        part = pl.ds(chunk * rows, rows)
        for cell in range(cells):
            out_ref[cell, part, :] = held_ref[part, cell, :]
    table_copy.wait()


def place_in_team():
    position = lax.axis_index("ax")
    core = lax.rem(position, jnp.int32(cores))
    chip = lax.div(position, jnp.int32(cores))
    return core, lax.rem(chip, jnp.int32(merge)), lax.div(chip, jnp.int32(merge))


def power(base, count):
    result = None
    while count:
        if count & 1:
            result = base if result is None else result * base
        base = base * base
        count >>= 1
    return result


def forward_kernel(table_ref, x_ref, out_ref):
    half_t = x_ref.shape[0] // 2
    width = x_ref.shape[1]
    blocks, size, _ = out_ref.shape
    low, high = x_ref[:half_t], x_ref[half_t:]
    for parity in range(2):
        folded = low + high if parity == 0 else low - high
        a, b, c = split3(folded)
        first = mul(table_ref[parity], twice(jnp.concatenate([a, b], axis=1), 0))
        result = first[:, :width] + (first[:, width:] + mul(table_ref[parity, :, :half_t], c))
        out_ref[:, parity * (size // 2) : (parity + 1) * (size // 2), :] = result.reshape(
            blocks, size // 2, width
        )


def backward_kernel(table_ref, x_ref, out_ref):
    blocks, size, width = x_ref.shape
    half_k = blocks * size // 2
    sums = []
    for parity in range(2):
        part = x_ref[:, parity * (size // 2) : (parity + 1) * (size // 2), :].reshape(-1, width)
        a, b = split2(part)
        first = mul(table_ref[parity, :, :half_k], jnp.concatenate([a, b], axis=1))
        sums.append(first[:, :width] + (first[:, width:] + mul(table_ref[parity, :, half_k:], a)))
    half_t = out_ref.shape[0] // 2
    out_ref[:half_t] = sums[0] + sums[1]
    out_ref[half_t:] = sums[0] - sums[1]


def modal_kernel(x_ref, basis_ref, weights_ref, decay_ref, f_ref, carry_ref):
    depth, size, _ = x_ref.shape
    weights = weights_ref[...]
    first = place_in_team()[1] * size
    for place in range(size):
        parity, half = divmod(place, size // 2)
        values = jnp.concatenate(split3(x_ref[:, place, :] * weights), axis=0)
        basis = jnp.concatenate(split2(basis_ref[first + (2 * half + parity)]), axis=0)
        result = mul(twice(values, 1), basis)
        f_ref[:, place, :] = result[:depth] + (result[depth : 2 * depth] + result[2 * depth :])
    decay = decay_ref[...]
    part = depth // merge
    ups = [f_ref[which * part] for which in range(merge)]
    downs = [f_ref[which * part + part - 1] for which in range(merge)]
    for step in range(1, part):
        for which in range(merge):
            ups[which] = ups[which] * decay + f_ref[which * part + step]
            downs[which] = downs[which] * decay + f_ref[which * part + part - 1 - step]
    for which in range(merge):
        carry_ref[which, 0] = ups[which]
        carry_ref[which, 1] = downs[which]


def solve_kernel(
    f_ref, basis_ref, decay_ref, gain_ref, link_ref, lead_ref, mix_ref, near_ref, end_ref, carry_ref, twin_ref, *refs
):
    *other_refs, out_ref, up_ref, down_ref = refs
    depth, size, _ = f_ref.shape
    part = depth // merge
    decay = decay_ref[...]
    first = place_in_team()[1] * size

    def within_team(target, end):
        terms = [
            link_ref[owner, target, source, end] * ref[source, end]
            for owner, ref in enumerate((carry_ref, twin_ref))
            for source in range(merge)
        ]
        return functools.reduce(jnp.add, terms)

    total = [within_team(merge, end) for end in range(2)]
    start = [jnp.zeros_like(decay)] * 2
    for turn, other_ref in enumerate(other_refs):
        other = [other_ref[0], other_ref[1]]
        start = [start[end] + near_ref[turn, end] * other[end] for end in range(2)]
        total = [mix_ref[turn, 0, end] * total[end] + mix_ref[turn, 1, end] * other[end] for end in range(2)]
    start = [start[end] + (end_ref[end, 0] * total[0] + end_ref[end, 1] * total[1]) for end in range(2)]
    ups, downs = (
        [within_team(which, end) + lead_ref[which, end] * start[end] for which in range(merge)] for end in range(2)
    )
    for step in range(part):
        for which in range(merge):
            low = which * part + step
            high = which * part + part - 1 - step
            ups[which] = ups[which] * decay
            up_ref[low] = ups[which]
            ups[which] = ups[which] + f_ref[low]
            downs[which] = downs[which] * decay + f_ref[high]
            down_ref[high] = downs[which]
    for place in range(size):
        parity, half = divmod(place, size // 2)
        field = (up_ref[:, place, :] + down_ref[:, place, :]) * gain_ref[place : place + 1, :]
        values = jnp.concatenate(split2(field), axis=0)
        basis = jnp.concatenate(split2(basis_ref[first + (2 * half + parity)]), axis=1)
        result = mul_t(twice(values, 1), basis)
        out_ref[:, place, :] = result[:depth] + result[depth:]


def scatter_kernel(x_ref, out_ref, row_sems):
    rows = [
        pltpu.make_async_copy(x_ref.at[cell], out_ref.at[:, cell], row_sems.at[cell])
        for cell in range(x_ref.shape[0])
    ]
    for copy in rows:
        copy.start()
    for copy in rows:
        copy.wait()


def whole(memory_space=pltpu.VMEM):
    return pl.BlockSpec(memory_space=memory_space)


def in_vmem(value):
    return pltpu.with_memory_space_constraint(value, pltpu.VMEM)


def in_hbm(value):
    return pltpu.with_memory_space_constraint(value, pltpu.HBM)


def body(source, radial_basis, radial_weights, mode_shifts):
    planes = lax.axis_size("plane")
    blocks = lax.axis_size("ax")
    local_t, depth_cells, radius_count = source.shape
    total_t = local_t * planes
    size = local_t // merge
    span = depth_cells * merge
    teams = blocks // (merge * cores)
    table = fourier_halves(total_t, planes, merge)
    forward_table = jnp.asarray(split_table(table))
    backward_table = jnp.asarray(split_table(table.transpose(0, 2, 1)))
    neighbours = [
        [
            plane * blocks + (team * merge + share) * cores + core
            for share in range(merge)
            for plane in range(planes)
        ]
        for team in range(teams)
        for core in range(cores)
    ]
    rounds = swaps(teams)

    turned, held_table, decay, gain, link, lead, mix, near, ends = pl.pallas_call(
        prepare_kernel,
        out_shape=(
            pltpu.VMEM((depth_cells, local_t, radius_count), f32),
            pltpu.VMEM(forward_table.shape, bf16),
            pltpu.VMEM((size, radius_count), f32),
            pltpu.VMEM((size, radius_count), f32),
            pltpu.VMEM((2, merge + 1, merge, 2, size, radius_count), f32),
            pltpu.VMEM((merge, 2, size, radius_count), f32),
            pltpu.VMEM((len(rounds), 2, 2, size, radius_count), f32),
            pltpu.VMEM((len(rounds), 2, size, radius_count), f32),
            pltpu.VMEM((2, 2, size, radius_count), f32),
        ),
        in_specs=[whole(pltpu.HBM)] * 3,
        out_specs=(whole(),) * 9,
        scratch_shapes=[
            pltpu.VMEM(source.shape, f32),
            pltpu.VMEM(mode_shifts.shape, f32),
            pltpu.SemaphoreType.DMA((4,)),
            pltpu.SemaphoreType.DMA((2,)),
        ],
        name="cells_first",
        compiler_params=compact,
    )(in_hbm(source), in_hbm(mode_shifts), in_hbm(forward_table))
    piece = lax.all_to_all(turned, "plane", 0, 0, tiled=True)
    spectral = pl.pallas_call(
        forward_kernel,
        out_shape=pltpu.VMEM((planes * merge, size, radius_count), f32),
        in_specs=[whole()] * 2,
        out_specs=whole(),
        name="fourier_forward",
        compiler_params=compact,
    )(in_vmem(held_table), in_vmem(piece.reshape(total_t, radius_count)))
    modal = lax.all_to_all(
        spectral, ("plane", "ax"), 0, 0, tiled=True, axis_index_groups=neighbours
    )
    spectra, carries = pl.pallas_call(
        modal_kernel,
        out_shape=(
            pltpu.VMEM((span, size, radius_count), f32),
            pltpu.VMEM((merge, 2, size, radius_count), f32),
        ),
        in_specs=[whole()] * 4,
        out_specs=(whole(), whole()),
        name="radial_forward",
        compiler_params=compact,
    )(in_vmem(modal), in_vmem(radial_basis), radial_weights.reshape(1, radius_count), in_vmem(decay))
    twin = lax.ppermute(carries, "ax", [(index, index ^ 1) for index in range(blocks)])
    sent = (link[0, merge] * carries + link[1, merge] * twin).sum(axis=0)
    others = []
    for turn, partners in enumerate(rounds):
        if turn:
            sent = mix[turn - 1, 0] * sent + mix[turn - 1, 1] * others[-1]
        width = merge * cores
        pairs = [
            (team * width + member, partner * width + member)
            for team, partner in enumerate(partners)
            for member in range(width)
        ]
        others.append(lax.ppermute(sent, "ax", pairs))
    radial_field = pl.pallas_call(
        solve_kernel,
        out_shape=pltpu.VMEM((span, size, radius_count), f32),
        in_specs=[whole()] * (11 + len(rounds)),
        out_specs=whole(),
        scratch_shapes=[pltpu.VMEM((span, size, radius_count), f32)] * 2,
        name="solve_and_radial_back",
        compiler_params=compact,
    )(
        in_vmem(spectra),
        in_vmem(radial_basis),
        in_vmem(decay),
        in_vmem(gain),
        in_vmem(link),
        in_vmem(lead),
        in_vmem(mix),
        in_vmem(near),
        in_vmem(ends),
        in_vmem(carries),
        in_vmem(twin),
        *map(in_vmem, others),
    )
    collected = lax.all_to_all(
        radial_field, ("plane", "ax"), 0, 0, tiled=True, axis_index_groups=neighbours
    )
    spatial = pl.pallas_call(
        backward_kernel,
        out_shape=pltpu.VMEM((total_t, radius_count), f32),
        in_specs=[whole()] * 2,
        out_specs=whole(),
        name="fourier_backward",
        compiler_params=compact,
    )(in_vmem(backward_table), in_vmem(collected))
    pressure = lax.all_to_all(
        spatial.reshape(planes, local_t, radius_count), "plane", 0, 0, tiled=True
    )
    return pl.pallas_call(
        scatter_kernel,
        out_shape=jax.ShapeDtypeStruct(source.shape, f32),
        in_specs=[whole()],
        out_specs=whole(pltpu.HBM),
        scratch_shapes=[pltpu.SemaphoreType.DMA((depth_cells,))],
        name="angles_first",
        compiler_params=compact,
    )(in_vmem(pressure))


def solution(mesh):
    placed = (P("plane", "ax", None), P("plane", None, None), P(), P("plane", None))
    return jax.shard_map(
        body, mesh=mesh, in_specs=placed, out_specs=P("plane", "ax", None), check_vma=False
    )
```

```python
import functools
import math

import jax
import jax.numpy as jnp
import numpy as np
from jax import lax
from jax.experimental import pallas as pl
from jax.experimental.pallas import tpu as pltpu
from jax.sharding import PartitionSpec as P

axial_scale = 0.01
cores = 2
merge = 2
bf16 = jnp.bfloat16
f32 = jnp.float32
compact = pltpu.CompilerParams(vmem_limit_bytes=16 * 2**20)


def mode_offset(place, size):
    quarter = size // 4
    if place < quarter:
        return 4 * place
    if place < 2 * quarter:
        return 4 * (place - quarter) + 2
    return 2 * (place - 2 * quarter) + 1


def fourier_parts(total, planes, share):
    local = total // planes
    size = local // share
    bounds = (0, size // 4, size // 2, size)
    tables = []
    for which, columns in enumerate((total // 4, total // 4, total // 2)):
        offsets = np.array([mode_offset(place, size) for place in range(bounds[which], bounds[which + 1])])
        share_at, plane_at, offset = np.meshgrid(np.arange(share), np.arange(planes), offsets, indexing="ij")
        order = (plane_at * local + share_at * size + offset).reshape(-1)
        middle = total // 2
        harmonic = np.where(order <= middle, order, order - middle)
        radians = (harmonic[:, None] * np.arange(columns) % total) * (2.0 * math.pi / total)
        factor = np.where((order == 0) | (order == middle), math.sqrt(1.0 / total), math.sqrt(2.0 / total))
        waves = np.where((order <= middle)[:, None], np.cos(radians), np.sin(radians))
        tables.append((waves * factor[:, None]).astype(np.float32))
    return np.stack(tables[:2]), tables[2][None]


def split2(value):
    high = value.astype(bf16)
    return high, (value - high.astype(f32)).astype(bf16)


def split3(value):
    high = value.astype(bf16)
    rest = value - high.astype(f32)
    middle = rest.astype(bf16)
    return high, middle, (rest - middle.astype(f32)).astype(bf16)


def mul(left, right):
    return jnp.dot(left, right, preferred_element_type=f32)


def mul_t(left, right):
    return lax.dot_general(left, right, (((1,), (1,)), ((), ())), preferred_element_type=f32)


def twice(value, axis):
    return jnp.concatenate([value, value], axis=axis)


def swap_tiles(from_ref, to_ref, firsts, seconds):
    for first in firsts:
        for second in seconds:
            rows, columns = slice(first, first + firsts.step), slice(second, second + seconds.step)
            to_ref[rows, columns, :] = jnp.swapaxes(from_ref[columns, rows, :], 0, 1)


def swaps(teams):
    rounds = []
    reach = 1
    while reach < teams:
        if 2 * reach == teams and teams == 4:
            rounds.append([team ^ 3 for team in range(teams)])
        elif 2 * reach == teams and teams >= 8:
            wide = teams // 8
            far = (6, 7, 4, 5, 2, 3, 0, 1)
            rounds.append([far[team // wide] * wide + team % wide for team in range(teams)])
        else:
            rounds.append([team ^ reach for team in range(teams)])
        reach *= 2
    return rounds


def prepare_kernel(
    source_ref, shifts_ref, even_ref, odd_ref, out_ref, even_out_ref, odd_out_ref, decay_ref, gain_ref, link_ref, lead_ref, mix_ref, near_ref, end_ref,
    held_ref, shift_ref, sems, extra_sems,
):
    cells, angles, _ = out_ref.shape
    size = decay_ref.shape[0]
    rounds = near_ref.shape[0]
    teams = 2**rounds
    chunks = sems.shape[0]
    rows = angles // chunks
    shift_copy = pltpu.make_async_copy(shifts_ref, shift_ref, extra_sems.at[0])
    table_copies = [
        pltpu.make_async_copy(even_ref, even_out_ref, extra_sems.at[1]),
        pltpu.make_async_copy(odd_ref, odd_out_ref, extra_sems.at[2]),
    ]
    copies = [
        pltpu.make_async_copy(
            source_ref.at[pl.ds(chunk * rows, rows)], held_ref.at[pl.ds(chunk * rows, rows)], sems.at[chunk]
        )
        for chunk in range(chunks)
    ]
    shift_copy.start()
    for copy in copies:
        copy.start()
    for copy in table_copies:
        copy.start()

    core, share, team = place_in_team()
    first = share * size
    shift_copy.wait()
    shifts = jnp.concatenate(
        [
            shift_ref[pl.ds(first, size // 4, stride=4), :],
            shift_ref[pl.ds(first + 2, size // 4, stride=4), :],
            shift_ref[pl.ds(first + 1, size // 2, stride=2), :],
        ],
        axis=0,
    )
    rise = 0.5 * jnp.sqrt((2.0 + shifts) - 2.0)
    cosh_half = jnp.sqrt(1.0 + rise * rise)
    root = cosh_half - rise
    decay = root * root
    decay_ref[...] = decay
    gain_ref[...] = axial_scale / (4.0 * rise * cosh_half)
    one = jnp.ones_like(decay)
    zero = jnp.zeros_like(decay)

    inner = [one, power(decay, cells)]
    for _ in range(2):
        inner.append(inner[-1] * inner[1])
    on_first = core == 0

    def apart(distance):
        below = inner[-distance - 1] if distance < 0 else zero
        above = inner[distance - 1] if distance > 0 else zero
        return below, above

    for source in range(merge):
        for target in range(merge):
            gap = 2 * (source - target)
            for end in range(2):
                link_ref[0, target, source, end] = apart(gap)[end]
                link_ref[1, target, source, end] = jnp.where(
                    on_first, apart(gap + 1)[end], apart(gap - 1)[end]
                )
        early, late = 2 * source, 2 * source + 1
        for owner in range(2):
            near, far = (early, late) if owner == 0 else (late, early)
            link_ref[owner, merge, source, 0] = jnp.where(on_first, inner[3 - near], inner[3 - far])
            link_ref[owner, merge, source, 1] = jnp.where(on_first, inner[near], inner[far])
        lead_ref[source, 0] = jnp.where(on_first, inner[early], inner[late])
        lead_ref[source, 1] = jnp.where(on_first, inner[3 - early], inner[3 - late])

    powers = [inner[3] * inner[1]]
    for _ in range(rounds):
        powers.append(powers[-1] * powers[-1])
    whole_decay = powers[-1] * decay

    def step_power(count, bits):
        result = one
        for bit in range(bits):
            result = jnp.where((count & (1 << bit)) != 0, result * powers[bit], result)
        return result

    for turn in range(rounds):
        reach = 1 << turn
        above = (team & reach) != 0
        offset = team & (reach - 1)
        mine = jnp.where(above, one, powers[turn])
        theirs = jnp.where(above, powers[turn], one)
        mix_ref[turn, 0, 0] = mine
        mix_ref[turn, 0, 1] = theirs
        mix_ref[turn, 1, 0] = theirs
        mix_ref[turn, 1, 1] = mine
        near_ref[turn, 0] = jnp.where(above, step_power(offset, turn), zero)
        near_ref[turn, 1] = jnp.where(above, zero, step_power(reach - 1 - offset, turn))
    closing = decay / (1.0 - whole_decay * whole_decay)
    to_first = closing * step_power(team, rounds)
    to_last = closing * step_power(teams - 1 - team, rounds)
    end_ref[0, 0] = to_first * whole_decay
    end_ref[0, 1] = -to_first
    end_ref[1, 0] = -to_last
    end_ref[1, 1] = to_last * whole_decay

    for chunk, copy in enumerate(copies):
        copy.wait()
        swap_tiles(held_ref, out_ref, range(0, cells, min(8, cells)), range(chunk * rows, (chunk + 1) * rows, min(8, rows)))
    for copy in table_copies:
        copy.wait()


def place_in_team():
    position = lax.axis_index("ax")
    core = lax.rem(position, jnp.int32(cores))
    chip = lax.div(position, jnp.int32(cores))
    return core, lax.rem(chip, jnp.int32(merge)), lax.div(chip, jnp.int32(merge))


def power(base, count):
    result = None
    while count:
        if count & 1:
            result = base if result is None else result * base
        base = base * base
        count >>= 1
    return result


def forward_kernel(even_ref, odd_ref, x_ref, out_ref):
    total, width = x_ref.shape
    blocks, size, _ = out_ref.shape
    half, quarter = total // 2, total // 4
    low, high = x_ref[:half], x_ref[half:]
    kept, turned = low + high, low - high
    parts = (
        (even_ref, 0, kept[:quarter] + kept[quarter:]),
        (even_ref, 1, kept[:quarter] - kept[quarter:]),
        (odd_ref, 0, turned),
    )
    at = 0
    for table_ref, which, folded in parts:
        rows = table_ref.shape[1] // blocks
        a, b, c = split3(folded)
        leading, rest = split2(table_ref[which])
        pair = jnp.concatenate([a, b], axis=1)
        first = mul(leading, pair) + mul(rest, pair)
        result = first[:, :width] + (first[:, width:] + mul(leading, c))
        out_ref[:, at : at + rows, :] = result.reshape(blocks, rows, width)
        at += rows


def backward_kernel(even_ref, odd_ref, x_ref, out_ref):
    blocks, size, width = x_ref.shape
    total = out_ref.shape[0]
    half, quarter = total // 2, total // 4
    sums = []
    at = 0
    for table_ref, which in ((even_ref, 0), (even_ref, 1), (odd_ref, 0)):
        rows = table_ref.shape[2] // blocks
        a, b = split2(x_ref[:, at : at + rows, :].reshape(rows * blocks, width))
        leading, rest = split2(table_ref[which])
        first = mul(leading, jnp.concatenate([a, b], axis=1))
        sums.append(first[:, :width] + (first[:, width:] + mul(rest, a)))
        at += rows
    fours, twos, odd = sums
    for which, even in enumerate((fours + twos, fours - twos)):
        part = odd[which * quarter : (which + 1) * quarter]
        out_ref[which * quarter : (which + 1) * quarter] = even + part
        out_ref[half + which * quarter : half + (which + 1) * quarter] = even - part


def modal_kernel(x_ref, basis_ref, weights_ref, decay_ref, f_ref, carry_ref):
    depth, size, _ = x_ref.shape
    weights = weights_ref[...]
    first = place_in_team()[1] * size
    tile = min(8, size)
    for group in range(0, size, tile):
        rows = jnp.swapaxes(x_ref[:, group : group + tile, :] * weights, 0, 1)
        results = []
        for inner in range(tile):
            values = jnp.concatenate(split3(rows[inner]), axis=0)
            basis = jnp.concatenate(split2(basis_ref[first + mode_offset(group + inner, size)]), axis=0)
            result = mul(twice(values, 1), basis)
            results.append(result[:depth] + (result[depth : 2 * depth] + result[2 * depth :]))
        f_ref[:, group : group + tile, :] = jnp.swapaxes(jnp.stack(results), 0, 1)
    decay = decay_ref[...]
    part = depth // merge
    ups = [f_ref[which * part] for which in range(merge)]
    downs = [f_ref[which * part + part - 1] for which in range(merge)]
    for step in range(1, part):
        for which in range(merge):
            ups[which] = ups[which] * decay + f_ref[which * part + step]
            downs[which] = downs[which] * decay + f_ref[which * part + part - 1 - step]
    for which in range(merge):
        carry_ref[which, 0] = ups[which]
        carry_ref[which, 1] = downs[which]


def solve_kernel(
    f_ref, basis_ref, decay_ref, gain_ref, link_ref, lead_ref, mix_ref, near_ref, end_ref, carry_ref, twin_ref, *refs
):
    *other_refs, out_ref, up_ref, down_ref = refs
    depth, size, _ = f_ref.shape
    part = depth // merge
    decay = decay_ref[...]
    first = place_in_team()[1] * size

    def within_team(target, end):
        terms = [
            link_ref[owner, target, source, end] * ref[source, end]
            for owner, ref in enumerate((carry_ref, twin_ref))
            for source in range(merge)
        ]
        return functools.reduce(jnp.add, terms)

    total = [within_team(merge, end) for end in range(2)]
    start = [jnp.zeros_like(decay)] * 2
    for turn, other_ref in enumerate(other_refs):
        other = [other_ref[0], other_ref[1]]
        start = [start[end] + near_ref[turn, end] * other[end] for end in range(2)]
        total = [mix_ref[turn, 0, end] * total[end] + mix_ref[turn, 1, end] * other[end] for end in range(2)]
    start = [start[end] + (end_ref[end, 0] * total[0] + end_ref[end, 1] * total[1]) for end in range(2)]
    ups, downs = (
        [within_team(which, end) + lead_ref[which, end] * start[end] for which in range(merge)] for end in range(2)
    )
    for step in range(part):
        for which in range(merge):
            low = which * part + step
            high = which * part + part - 1 - step
            ups[which] = ups[which] * decay
            up_ref[low] = ups[which]
            ups[which] = ups[which] + f_ref[low]
            downs[which] = downs[which] * decay + f_ref[high]
            down_ref[high] = downs[which]
    tile = min(8, size)
    for group in range(0, size, tile):
        part = slice(group, group + tile)
        rows = jnp.swapaxes((up_ref[:, part, :] + down_ref[:, part, :]) * gain_ref[part, :], 0, 1)
        results = []
        for inner in range(tile):
            values = jnp.concatenate(split2(rows[inner]), axis=0)
            basis = jnp.concatenate(split2(basis_ref[first + mode_offset(group + inner, size)]), axis=1)
            result = mul_t(twice(values, 1), basis)
            results.append(result[:depth] + result[depth:])
        out_ref[:, part, :] = jnp.swapaxes(jnp.stack(results), 0, 1)


def scatter_kernel(x_ref, out_ref, turned_ref, sems):
    cells, angles, _ = x_ref.shape
    chunks = sems.shape[0]
    rows = angles // chunks
    copies = []
    for chunk in range(chunks):
        swap_tiles(x_ref, turned_ref, range(chunk * rows, (chunk + 1) * rows, min(8, rows)), range(0, cells, min(8, cells)))
        part = pl.ds(chunk * rows, rows)
        copies.append(pltpu.make_async_copy(turned_ref.at[part], out_ref.at[part], sems.at[chunk]))
        copies[-1].start()
    for copy in copies:
        copy.wait()


def whole(memory_space=pltpu.VMEM):
    return pl.BlockSpec(memory_space=memory_space)


def in_vmem(value):
    return pltpu.with_memory_space_constraint(value, pltpu.VMEM)


def in_hbm(value):
    return pltpu.with_memory_space_constraint(value, pltpu.HBM)


def body(source, radial_basis, radial_weights, mode_shifts):
    planes = lax.axis_size("plane")
    blocks = lax.axis_size("ax")
    local_t, depth_cells, radius_count = source.shape
    total_t = local_t * planes
    size = local_t // merge
    span = depth_cells * merge
    teams = blocks // (merge * cores)
    tables = fourier_parts(total_t, planes, merge)
    forward_tables = [jnp.asarray(table) for table in tables]
    backward_tables = [jnp.asarray(table.transpose(0, 2, 1)) for table in tables]
    neighbours = [
        [
            plane * blocks + (team * merge + share) * cores + core
            for share in range(merge)
            for plane in range(planes)
        ]
        for team in range(teams)
        for core in range(cores)
    ]
    rounds = swaps(teams)

    turned, held_even, held_odd, decay, gain, link, lead, mix, near, ends = pl.pallas_call(
        prepare_kernel,
        out_shape=(
            pltpu.VMEM((depth_cells, local_t, radius_count), f32),
            *(pltpu.VMEM(table.shape, f32) for table in forward_tables),
            pltpu.VMEM((size, radius_count), f32),
            pltpu.VMEM((size, radius_count), f32),
            pltpu.VMEM((2, merge + 1, merge, 2, size, radius_count), f32),
            pltpu.VMEM((merge, 2, size, radius_count), f32),
            pltpu.VMEM((len(rounds), 2, 2, size, radius_count), f32),
            pltpu.VMEM((len(rounds), 2, size, radius_count), f32),
            pltpu.VMEM((2, 2, size, radius_count), f32),
        ),
        in_specs=[whole(pltpu.HBM)] * 4,
        out_specs=(whole(),) * 10,
        scratch_shapes=[
            pltpu.VMEM(source.shape, f32),
            pltpu.VMEM(mode_shifts.shape, f32),
            pltpu.SemaphoreType.DMA((2,)),
            pltpu.SemaphoreType.DMA((3,)),
        ],
        name="cells_first",
        compiler_params=compact,
    )(in_hbm(source), in_hbm(mode_shifts), *map(in_hbm, forward_tables))
    piece = lax.all_to_all(turned, "plane", 0, 0, tiled=True)
    spectral = pl.pallas_call(
        forward_kernel,
        out_shape=pltpu.VMEM((planes * merge, size, radius_count), f32),
        in_specs=[whole()] * 3,
        out_specs=whole(),
        name="fourier_forward",
        compiler_params=compact,
    )(in_vmem(held_even), in_vmem(held_odd), in_vmem(piece.reshape(total_t, radius_count)))
    modal = lax.all_to_all(
        spectral, ("plane", "ax"), 0, 0, tiled=True, axis_index_groups=neighbours
    )
    spectra, carries = pl.pallas_call(
        modal_kernel,
        out_shape=(
            pltpu.VMEM((span, size, radius_count), f32),
            pltpu.VMEM((merge, 2, size, radius_count), f32),
        ),
        in_specs=[whole()] * 4,
        out_specs=(whole(), whole()),
        name="radial_forward",
        compiler_params=compact,
    )(in_vmem(modal), in_vmem(radial_basis), radial_weights.reshape(1, radius_count), in_vmem(decay))
    twin = lax.ppermute(carries, "ax", [(index, index ^ 1) for index in range(blocks)])
    sent = (link[0, merge] * carries + link[1, merge] * twin).sum(axis=0)
    others = []
    for turn, partners in enumerate(rounds):
        if turn:
            sent = mix[turn - 1, 0] * sent + mix[turn - 1, 1] * others[-1]
        width = merge * cores
        pairs = [
            (team * width + member, partner * width + member)
            for team, partner in enumerate(partners)
            for member in range(width)
        ]
        others.append(lax.ppermute(sent, "ax", pairs))
    radial_field = pl.pallas_call(
        solve_kernel,
        out_shape=pltpu.VMEM((span, size, radius_count), f32),
        in_specs=[whole()] * (11 + len(rounds)),
        out_specs=whole(),
        scratch_shapes=[pltpu.VMEM((span, size, radius_count), f32)] * 2,
        name="solve_and_radial_back",
        compiler_params=compact,
    )(
        in_vmem(spectra),
        in_vmem(radial_basis),
        in_vmem(decay),
        in_vmem(gain),
        in_vmem(link),
        in_vmem(lead),
        in_vmem(mix),
        in_vmem(near),
        in_vmem(ends),
        in_vmem(carries),
        in_vmem(twin),
        *map(in_vmem, others),
    )
    collected = lax.all_to_all(
        radial_field, ("plane", "ax"), 0, 0, tiled=True, axis_index_groups=neighbours
    )
    spatial = pl.pallas_call(
        backward_kernel,
        out_shape=pltpu.VMEM((total_t, radius_count), f32),
        in_specs=[whole()] * 3,
        out_specs=whole(),
        name="fourier_backward",
        compiler_params=compact,
    )(*map(in_vmem, backward_tables), in_vmem(collected))
    pressure = lax.all_to_all(
        spatial.reshape(planes, local_t, radius_count), "plane", 0, 0, tiled=True
    )
    return pl.pallas_call(
        scatter_kernel,
        out_shape=jax.ShapeDtypeStruct(source.shape, f32),
        in_specs=[whole()],
        out_specs=whole(pltpu.HBM),
        scratch_shapes=[pltpu.VMEM(source.shape, f32), pltpu.SemaphoreType.DMA((4,))],
        name="angles_first",
        compiler_params=compact,
    )(in_vmem(pressure))


def solution(mesh):
    placed = (P("plane", "ax", None), P("plane", None, None), P(), P("plane", None))
    return jax.shard_map(
        body, mesh=mesh, in_specs=placed, out_specs=P("plane", "ax", None), check_vma=False
    )
```

```python
import functools
import math

import jax
import jax.numpy as jnp
import numpy as np
from jax import lax
from jax.experimental import pallas as pl
from jax.experimental.pallas import tpu as pltpu
from jax.sharding import PartitionSpec as P

axial_scale = 0.01
cores = 2
merge = 2
bf16 = jnp.bfloat16
f32 = jnp.float32
compact = pltpu.CompilerParams(vmem_limit_bytes=16 * 2**20)


def mode_offset(place, size):
    quarter = size // 4
    if place < quarter:
        return 4 * place
    if place < 2 * quarter:
        return 4 * (place - quarter) + 2
    return 2 * (place - 2 * quarter) + 1


def fourier_parts(total, planes, share):
    local = total // planes
    size = local // share
    bounds = (0, size // 4, size // 2, size)
    tables = []
    for which, columns in enumerate((total // 4, total // 4, total // 2)):
        offsets = np.array([mode_offset(place, size) for place in range(bounds[which], bounds[which + 1])])
        share_at, plane_at, offset = np.meshgrid(np.arange(share), np.arange(planes), offsets, indexing="ij")
        order = (plane_at * local + share_at * size + offset).reshape(-1)
        middle = total // 2
        harmonic = np.where(order <= middle, order, order - middle)
        radians = (harmonic[:, None] * np.arange(columns) % total) * (2.0 * math.pi / total)
        factor = np.where((order == 0) | (order == middle), math.sqrt(1.0 / total), math.sqrt(2.0 / total))
        waves = np.where((order <= middle)[:, None], np.cos(radians), np.sin(radians))
        tables.append((waves * factor[:, None]).astype(np.float32))
    return np.stack(tables[:2]), tables[2][None]


def split2(value):
    high = value.astype(bf16)
    return high, (value - high.astype(f32)).astype(bf16)


def split3(value):
    high = value.astype(bf16)
    rest = value - high.astype(f32)
    middle = rest.astype(bf16)
    return high, middle, (rest - middle.astype(f32)).astype(bf16)


def mul(left, right):
    return jnp.dot(left, right, preferred_element_type=f32)


def mul_t(left, right):
    return lax.dot_general(left, right, (((1,), (1,)), ((), ())), preferred_element_type=f32)


def twice(value, axis):
    return jnp.concatenate([value, value], axis=axis)


def swap_tiles(from_ref, to_ref, firsts, seconds):
    for first in firsts:
        for second in seconds:
            rows, columns = slice(first, first + firsts.step), slice(second, second + seconds.step)
            to_ref[rows, columns, :] = jnp.swapaxes(from_ref[columns, rows, :], 0, 1)


def swaps(teams):
    rounds = []
    reach = 1
    while reach < teams:
        if 2 * reach == teams and teams == 4:
            rounds.append([team ^ 3 for team in range(teams)])
        elif 2 * reach == teams and teams >= 8:
            wide = teams // 8
            far = (6, 7, 4, 5, 2, 3, 0, 1)
            rounds.append([far[team // wide] * wide + team % wide for team in range(teams)])
        else:
            rounds.append([team ^ reach for team in range(teams)])
        reach *= 2
    return rounds


def prepare_kernel(
    source_ref, shifts_ref, even_ref, odd_ref, out_ref, even_out_ref, odd_out_ref, decay_ref, gain_ref, link_ref, lead_ref, mix_ref, near_ref, end_ref,
    held_ref, shift_ref, sems, extra_sems,
):
    cells, angles, _ = out_ref.shape
    size = decay_ref.shape[0]
    rounds = near_ref.shape[0]
    teams = 2**rounds
    chunks = sems.shape[0]
    rows = angles // chunks
    shift_copy = pltpu.make_async_copy(
        shifts_ref, shift_ref.at[pl.ds(0, shifts_ref.shape[0])], extra_sems.at[0]
    )
    table_copies = [
        pltpu.make_async_copy(even_ref, even_out_ref, extra_sems.at[1]),
        pltpu.make_async_copy(odd_ref, odd_out_ref, extra_sems.at[2]),
    ]
    copies = [
        pltpu.make_async_copy(
            source_ref.at[pl.ds(chunk * rows, rows)], held_ref.at[pl.ds(chunk * rows, rows)], sems.at[chunk]
        )
        for chunk in range(chunks)
    ]
    shift_copy.start()
    for copy in copies:
        copy.start()
    for copy in table_copies:
        copy.start()

    core, share, team = place_in_team()
    first = share * size
    shift_copy.wait()
    shifts = jnp.concatenate(
        [
            shift_ref[pl.ds(first, size // 4, stride=4), :],
            shift_ref[pl.ds(first + 2, size // 4, stride=4), :],
            shift_ref[pl.ds(first + 1, size // 2, stride=2), :],
        ],
        axis=0,
    )
    rise = 0.5 * jnp.sqrt((2.0 + shifts) - 2.0)
    cosh_half = jnp.sqrt(1.0 + rise * rise)
    root = cosh_half - rise
    decay = root * root
    decay_ref[...] = decay
    gain_ref[...] = axial_scale / (4.0 * rise * cosh_half)
    one = jnp.ones_like(decay)
    zero = jnp.zeros_like(decay)

    inner = [one, power(decay, cells)]
    for _ in range(2):
        inner.append(inner[-1] * inner[1])
    on_first = core == 0

    def apart(distance):
        below = inner[-distance - 1] if distance < 0 else zero
        above = inner[distance - 1] if distance > 0 else zero
        return below, above

    for source in range(merge):
        for target in range(merge):
            gap = 2 * (source - target)
            for end in range(2):
                link_ref[0, target, source, end] = apart(gap)[end]
                link_ref[1, target, source, end] = jnp.where(
                    on_first, apart(gap + 1)[end], apart(gap - 1)[end]
                )
        early, late = 2 * source, 2 * source + 1
        for owner in range(2):
            near, far = (early, late) if owner == 0 else (late, early)
            link_ref[owner, merge, source, 0] = jnp.where(on_first, inner[3 - near], inner[3 - far])
            link_ref[owner, merge, source, 1] = jnp.where(on_first, inner[near], inner[far])
        lead_ref[source, 0] = jnp.where(on_first, inner[early], inner[late])
        lead_ref[source, 1] = jnp.where(on_first, inner[3 - early], inner[3 - late])

    powers = [inner[3] * inner[1]]
    for _ in range(rounds):
        powers.append(powers[-1] * powers[-1])
    whole_decay = powers[-1] * decay

    def step_power(count, bits):
        result = one
        for bit in range(bits):
            result = jnp.where((count & (1 << bit)) != 0, result * powers[bit], result)
        return result

    for turn in range(rounds):
        reach = 1 << turn
        above = (team & reach) != 0
        offset = team & (reach - 1)
        mine = jnp.where(above, one, powers[turn])
        theirs = jnp.where(above, powers[turn], one)
        mix_ref[turn, 0, 0] = mine
        mix_ref[turn, 0, 1] = theirs
        mix_ref[turn, 1, 0] = theirs
        mix_ref[turn, 1, 1] = mine
        near_ref[turn, 0] = jnp.where(above, step_power(offset, turn), zero)
        near_ref[turn, 1] = jnp.where(above, zero, step_power(reach - 1 - offset, turn))
    closing = decay / (1.0 - whole_decay * whole_decay)
    to_first = closing * step_power(team, rounds)
    to_last = closing * step_power(teams - 1 - team, rounds)
    end_ref[0, 0] = to_first * whole_decay
    end_ref[0, 1] = -to_first
    end_ref[1, 0] = -to_last
    end_ref[1, 1] = to_last * whole_decay

    for chunk, copy in enumerate(copies):
        copy.wait()
        swap_tiles(held_ref, out_ref, range(0, cells, min(8, cells)), range(chunk * rows, (chunk + 1) * rows, min(8, rows)))
    for copy in table_copies:
        copy.wait()


def place_in_team():
    position = lax.axis_index("ax")
    core = lax.rem(position, jnp.int32(cores))
    chip = lax.div(position, jnp.int32(cores))
    return core, lax.rem(chip, jnp.int32(merge)), lax.div(chip, jnp.int32(merge))


def power(base, count):
    result = None
    while count:
        if count & 1:
            result = base if result is None else result * base
        base = base * base
        count >>= 1
    return result


def forward_kernel(even_ref, odd_ref, x_ref, out_ref):
    total, width = x_ref.shape
    blocks, size, _ = out_ref.shape
    half, quarter = total // 2, total // 4
    low, high = x_ref[:half], x_ref[half:]
    kept, turned = low + high, low - high
    parts = (
        (even_ref, 0, kept[:quarter] + kept[quarter:]),
        (even_ref, 1, kept[:quarter] - kept[quarter:]),
        (odd_ref, 0, turned),
    )
    at = 0
    for table_ref, which, folded in parts:
        rows = table_ref.shape[1] // blocks
        a, b, c = split3(folded)
        leading, rest = split2(table_ref[which])
        pair = jnp.concatenate([a, b], axis=1)
        first = mul(leading, pair) + mul(rest, pair)
        result = first[:, :width] + (first[:, width:] + mul(leading, c))
        out_ref[:, at : at + rows, :] = result.reshape(blocks, rows, width)
        at += rows


def backward_kernel(even_ref, odd_ref, x_ref, out_ref):
    blocks, size, width = x_ref.shape
    total = out_ref.shape[0]
    half, quarter = total // 2, total // 4
    sums = []
    at = 0
    for table_ref, which in ((even_ref, 0), (even_ref, 1), (odd_ref, 0)):
        rows = table_ref.shape[2] // blocks
        a, b = split2(x_ref[:, at : at + rows, :].reshape(rows * blocks, width))
        leading, rest = split2(table_ref[which])
        first = mul(leading, jnp.concatenate([a, b], axis=1))
        sums.append(first[:, :width] + (first[:, width:] + mul(rest, a)))
        at += rows
    fours, twos, odd = sums
    for which, even in enumerate((fours + twos, fours - twos)):
        part = odd[which * quarter : (which + 1) * quarter]
        out_ref[which * quarter : (which + 1) * quarter] = even + part
        out_ref[half + which * quarter : half + (which + 1) * quarter] = even - part


def modal_kernel(x_ref, basis_ref, weights_ref, decay_ref, f_ref, carry_ref):
    depth, size, _ = x_ref.shape
    weights = weights_ref[...]
    first = place_in_team()[1] * size
    tile = min(8, size)
    for group in range(0, size, tile):
        rows = jnp.swapaxes(x_ref[:, group : group + tile, :] * weights, 0, 1)
        results = []
        for inner in range(tile):
            values = jnp.concatenate(split3(rows[inner]), axis=0)
            basis = jnp.concatenate(split2(basis_ref[first + mode_offset(group + inner, size)]), axis=0)
            result = mul(twice(values, 1), basis)
            results.append(result[:depth] + (result[depth : 2 * depth] + result[2 * depth :]))
        f_ref[:, group : group + tile, :] = jnp.swapaxes(jnp.stack(results), 0, 1)
    decay = decay_ref[...]
    part = depth // merge
    ups = [f_ref[which * part] for which in range(merge)]
    downs = [f_ref[which * part + part - 1] for which in range(merge)]
    for step in range(1, part):
        for which in range(merge):
            ups[which] = ups[which] * decay + f_ref[which * part + step]
            downs[which] = downs[which] * decay + f_ref[which * part + part - 1 - step]
    for which in range(merge):
        carry_ref[which, 0] = ups[which]
        carry_ref[which, 1] = downs[which]


def solve_kernel(
    f_ref, basis_ref, decay_ref, gain_ref, link_ref, lead_ref, mix_ref, near_ref, end_ref, carry_ref, twin_ref, *refs
):
    *other_refs, out_ref, up_ref, down_ref = refs
    depth, size, _ = f_ref.shape
    part = depth // merge
    decay = decay_ref[...]
    first = place_in_team()[1] * size

    def within_team(target, end):
        terms = [
            link_ref[owner, target, source, end] * ref[source, end]
            for owner, ref in enumerate((carry_ref, twin_ref))
            for source in range(merge)
        ]
        return functools.reduce(jnp.add, terms)

    total = [within_team(merge, end) for end in range(2)]
    start = [jnp.zeros_like(decay)] * 2
    for turn, other_ref in enumerate(other_refs):
        other = [other_ref[0], other_ref[1]]
        start = [start[end] + near_ref[turn, end] * other[end] for end in range(2)]
        total = [mix_ref[turn, 0, end] * total[end] + mix_ref[turn, 1, end] * other[end] for end in range(2)]
    start = [start[end] + (end_ref[end, 0] * total[0] + end_ref[end, 1] * total[1]) for end in range(2)]
    ups, downs = (
        [within_team(which, end) + lead_ref[which, end] * start[end] for which in range(merge)] for end in range(2)
    )
    for step in range(part):
        for which in range(merge):
            low = which * part + step
            high = which * part + part - 1 - step
            ups[which] = ups[which] * decay
            up_ref[low] = ups[which]
            ups[which] = ups[which] + f_ref[low]
            downs[which] = downs[which] * decay + f_ref[high]
            down_ref[high] = downs[which]
    tile = min(8, size)
    for group in range(0, size, tile):
        part = slice(group, group + tile)
        rows = jnp.swapaxes((up_ref[:, part, :] + down_ref[:, part, :]) * gain_ref[part, :], 0, 1)
        results = []
        for inner in range(tile):
            values = jnp.concatenate(split2(rows[inner]), axis=0)
            basis = jnp.concatenate(split2(basis_ref[first + mode_offset(group + inner, size)]), axis=1)
            result = mul_t(twice(values, 1), basis)
            results.append(result[:depth] + result[depth:])
        out_ref[:, part, :] = jnp.swapaxes(jnp.stack(results), 0, 1)


def scatter_kernel(x_ref, out_ref, turned_ref, sems):
    cells, angles, _ = x_ref.shape
    chunks = sems.shape[0]
    rows = angles // chunks
    copies = []
    for chunk in range(chunks):
        swap_tiles(x_ref, turned_ref, range(chunk * rows, (chunk + 1) * rows, min(8, rows)), range(0, cells, min(8, cells)))
        part = pl.ds(chunk * rows, rows)
        copies.append(pltpu.make_async_copy(turned_ref.at[part], out_ref.at[part], sems.at[chunk]))
        copies[-1].start()
    for copy in copies:
        copy.wait()


def whole(memory_space=pltpu.VMEM):
    return pl.BlockSpec(memory_space=memory_space)


def in_vmem(value):
    return pltpu.with_memory_space_constraint(value, pltpu.VMEM)


def in_hbm(value):
    return pltpu.with_memory_space_constraint(value, pltpu.HBM)


def body(source, radial_basis, radial_weights, mode_shifts):
    planes = lax.axis_size("plane")
    blocks = lax.axis_size("ax")
    local_t, depth_cells, radius_count = source.shape
    total_t = local_t * planes
    size = local_t // merge
    span = depth_cells * merge
    teams = blocks // (merge * cores)
    tables = fourier_parts(total_t, planes, merge)
    forward_tables = [jnp.asarray(table) for table in tables]
    backward_tables = [jnp.asarray(table.transpose(0, 2, 1)) for table in tables]
    neighbours = [
        [
            plane * blocks + (team * merge + share) * cores + core
            for share in range(merge)
            for plane in range(planes)
        ]
        for team in range(teams)
        for core in range(cores)
    ]
    rounds = swaps(teams)

    turned, held_even, held_odd, decay, gain, link, lead, mix, near, ends = pl.pallas_call(
        prepare_kernel,
        out_shape=(
            pltpu.VMEM((depth_cells, local_t, radius_count), f32),
            *(pltpu.VMEM(table.shape, f32) for table in forward_tables),
            pltpu.VMEM((size, radius_count), f32),
            pltpu.VMEM((size, radius_count), f32),
            pltpu.VMEM((2, merge + 1, merge, 2, size, radius_count), f32),
            pltpu.VMEM((merge, 2, size, radius_count), f32),
            pltpu.VMEM((len(rounds), 2, 2, size, radius_count), f32),
            pltpu.VMEM((len(rounds), 2, size, radius_count), f32),
            pltpu.VMEM((2, 2, size, radius_count), f32),
        ),
        in_specs=[whole(pltpu.HBM)] * 4,
        out_specs=(whole(),) * 10,
        scratch_shapes=[
            pltpu.VMEM(source.shape, f32),
            pltpu.VMEM((local_t + 8, radius_count), f32),
            pltpu.SemaphoreType.DMA((2,)),
            pltpu.SemaphoreType.DMA((3,)),
        ],
        name="cells_first",
        compiler_params=compact,
    )(in_hbm(source), in_hbm(mode_shifts), *map(in_hbm, forward_tables))
    piece = lax.all_to_all(turned, "plane", 0, 0, tiled=True)
    spectral = pl.pallas_call(
        forward_kernel,
        out_shape=pltpu.VMEM((planes * merge, size, radius_count), f32),
        in_specs=[whole()] * 3,
        out_specs=whole(),
        name="fourier_forward",
        compiler_params=compact,
    )(in_vmem(held_even), in_vmem(held_odd), in_vmem(piece.reshape(total_t, radius_count)))
    modal = lax.all_to_all(
        spectral, ("plane", "ax"), 0, 0, tiled=True, axis_index_groups=neighbours
    )
    spectra, carries = pl.pallas_call(
        modal_kernel,
        out_shape=(
            pltpu.VMEM((span, size, radius_count), f32),
            pltpu.VMEM((merge, 2, size, radius_count), f32),
        ),
        in_specs=[whole()] * 4,
        out_specs=(whole(), whole()),
        name="radial_forward",
        compiler_params=compact,
    )(in_vmem(modal), in_vmem(radial_basis), radial_weights.reshape(1, radius_count), in_vmem(decay))
    twin = lax.ppermute(carries, "ax", [(index, index ^ 1) for index in range(blocks)])
    sent = (link[0, merge] * carries + link[1, merge] * twin).sum(axis=0)
    others = []
    for turn, partners in enumerate(rounds):
        if turn:
            sent = mix[turn - 1, 0] * sent + mix[turn - 1, 1] * others[-1]
        width = merge * cores
        pairs = [
            (team * width + member, partner * width + member)
            for team, partner in enumerate(partners)
            for member in range(width)
        ]
        others.append(lax.ppermute(sent, "ax", pairs))
    radial_field = pl.pallas_call(
        solve_kernel,
        out_shape=pltpu.VMEM((span, size, radius_count), f32),
        in_specs=[whole()] * (11 + len(rounds)),
        out_specs=whole(),
        scratch_shapes=[pltpu.VMEM((span, size, radius_count), f32)] * 2,
        name="solve_and_radial_back",
        compiler_params=compact,
    )(
        in_vmem(spectra),
        in_vmem(radial_basis),
        in_vmem(decay),
        in_vmem(gain),
        in_vmem(link),
        in_vmem(lead),
        in_vmem(mix),
        in_vmem(near),
        in_vmem(ends),
        in_vmem(carries),
        in_vmem(twin),
        *map(in_vmem, others),
    )
    collected = lax.all_to_all(
        radial_field, ("plane", "ax"), 0, 0, tiled=True, axis_index_groups=neighbours
    )
    spatial = pl.pallas_call(
        backward_kernel,
        out_shape=pltpu.VMEM((total_t, radius_count), f32),
        in_specs=[whole()] * 3,
        out_specs=whole(),
        name="fourier_backward",
        compiler_params=compact,
    )(*map(in_vmem, backward_tables), in_vmem(collected))
    pressure = lax.all_to_all(
        spatial.reshape(planes, local_t, radius_count), "plane", 0, 0, tiled=True
    )
    return pl.pallas_call(
        scatter_kernel,
        out_shape=jax.ShapeDtypeStruct(source.shape, f32),
        in_specs=[whole()],
        out_specs=whole(pltpu.HBM),
        scratch_shapes=[pltpu.VMEM(source.shape, f32), pltpu.SemaphoreType.DMA((4,))],
        name="angles_first",
        compiler_params=compact,
    )(in_vmem(pressure))


def solution(mesh):
    placed = (P("plane", "ax", None), P("plane", None, None), P(), P("plane", None))
    return jax.shard_map(
        body, mesh=mesh, in_specs=placed, out_specs=P("plane", "ax", None), check_vma=False
    )
```

```python
import functools
import math

import jax
import jax.numpy as jnp
import numpy as np
from jax import lax
from jax.experimental import pallas as pl
from jax.experimental.pallas import tpu as pltpu
from jax.sharding import PartitionSpec as P

axial_scale = 0.01
cores = 2
merge = 2
bf16 = jnp.bfloat16
f32 = jnp.float32
compact = pltpu.CompilerParams(vmem_limit_bytes=16 * 2**20)


def mode_offset(place, size):
    quarter = size // 4
    if place < quarter:
        return 4 * place
    if place < 2 * quarter:
        return 4 * (place - quarter) + 2
    return 2 * (place - 2 * quarter) + 1


def fourier_parts(total, planes, share):
    local = total // planes
    size = local // share
    bounds = (0, size // 4, size // 2, size)
    tables = []
    for which, columns in enumerate((total // 4, total // 4, total // 2)):
        offsets = np.array([mode_offset(place, size) for place in range(bounds[which], bounds[which + 1])])
        share_at, plane_at, offset = np.meshgrid(np.arange(share), np.arange(planes), offsets, indexing="ij")
        order = (plane_at * local + share_at * size + offset).reshape(-1)
        middle = total // 2
        harmonic = np.where(order <= middle, order, order - middle)
        radians = (harmonic[:, None] * np.arange(columns) % total) * (2.0 * math.pi / total)
        factor = np.where((order == 0) | (order == middle), math.sqrt(1.0 / total), math.sqrt(2.0 / total))
        waves = np.where((order <= middle)[:, None], np.cos(radians), np.sin(radians))
        tables.append((waves * factor[:, None]).astype(np.float32))
    return np.stack(tables[:2]), tables[2][None]


def split2(value):
    high = value.astype(bf16)
    return high, (value - high.astype(f32)).astype(bf16)


def split3(value):
    high = value.astype(bf16)
    rest = value - high.astype(f32)
    middle = rest.astype(bf16)
    return high, middle, (rest - middle.astype(f32)).astype(bf16)


def mul(left, right):
    return jnp.dot(left, right, preferred_element_type=f32)


def mul_t(left, right):
    return lax.dot_general(left, right, (((1,), (1,)), ((), ())), preferred_element_type=f32)


def twice(value, axis):
    return jnp.concatenate([value, value], axis=axis)


def swap_tiles(from_ref, to_ref, firsts, seconds):
    for first in firsts:
        for second in seconds:
            rows, columns = slice(first, first + firsts.step), slice(second, second + seconds.step)
            to_ref[rows, columns, :] = jnp.swapaxes(from_ref[columns, rows, :], 0, 1)


def swaps(teams):
    rounds = []
    reach = 1
    while reach < teams:
        if 2 * reach == teams and teams == 4:
            rounds.append([team ^ 3 for team in range(teams)])
        elif 2 * reach == teams and teams >= 8:
            wide = teams // 8
            far = (6, 7, 4, 5, 2, 3, 0, 1)
            rounds.append([far[team // wide] * wide + team % wide for team in range(teams)])
        else:
            rounds.append([team ^ reach for team in range(teams)])
        reach *= 2
    return rounds


def prepare_kernel(
    source_ref, shifts_ref, even_ref, odd_ref, out_ref, even_out_ref, odd_out_ref, decay_ref, gain_ref,
    held_ref, shift_ref, sems, extra_sems,
):
    cells, angles, _ = out_ref.shape
    size = decay_ref.shape[0]
    chunks = sems.shape[0]
    rows = angles // chunks
    shift_copy = pltpu.make_async_copy(
        shifts_ref, shift_ref.at[pl.ds(0, shifts_ref.shape[0])], extra_sems.at[0]
    )
    table_copies = [
        pltpu.make_async_copy(even_ref, even_out_ref, extra_sems.at[1]),
        pltpu.make_async_copy(odd_ref, odd_out_ref, extra_sems.at[2]),
    ]
    copies = [
        pltpu.make_async_copy(
            source_ref.at[pl.ds(chunk * rows, rows)], held_ref.at[pl.ds(chunk * rows, rows)], sems.at[chunk]
        )
        for chunk in range(chunks)
    ]
    shift_copy.start()
    for copy in copies:
        copy.start()
    for copy in table_copies:
        copy.start()

    first = place_in_team()[1] * size
    shift_copy.wait()
    shifts = jnp.concatenate(
        [
            shift_ref[pl.ds(first, size // 4, stride=4), :],
            shift_ref[pl.ds(first + 2, size // 4, stride=4), :],
            shift_ref[pl.ds(first + 1, size // 2, stride=2), :],
        ],
        axis=0,
    )
    rise = 0.5 * jnp.sqrt((2.0 + shifts) - 2.0)
    cosh_half = jnp.sqrt(1.0 + rise * rise)
    root = cosh_half - rise
    decay = root * root
    decay_ref[...] = decay
    gain_ref[...] = axial_scale / (4.0 * rise * cosh_half)
    for chunk, copy in enumerate(copies):
        copy.wait()
        swap_tiles(held_ref, out_ref, range(0, cells, min(8, cells)), range(chunk * rows, (chunk + 1) * rows, min(8, rows)))
    for copy in table_copies:
        copy.wait()


def factor_kernel(cells, decay_ref, link_ref, lead_ref, mix_ref, near_ref, end_ref):
    rounds = near_ref.shape[0]
    teams = 2**rounds
    core, _, team = place_in_team()
    decay = decay_ref[...]
    one = jnp.ones_like(decay)
    zero = jnp.zeros_like(decay)

    inner = [one, power(decay, cells)]
    for _ in range(2):
        inner.append(inner[-1] * inner[1])
    on_first = core == 0

    def apart(distance):
        below = inner[-distance - 1] if distance < 0 else zero
        above = inner[distance - 1] if distance > 0 else zero
        return below, above

    for source in range(merge):
        for target in range(merge):
            gap = 2 * (source - target)
            for end in range(2):
                link_ref[0, target, source, end] = apart(gap)[end]
                link_ref[1, target, source, end] = jnp.where(
                    on_first, apart(gap + 1)[end], apart(gap - 1)[end]
                )
        early, late = 2 * source, 2 * source + 1
        for owner in range(2):
            near, far = (early, late) if owner == 0 else (late, early)
            link_ref[owner, merge, source, 0] = jnp.where(on_first, inner[3 - near], inner[3 - far])
            link_ref[owner, merge, source, 1] = jnp.where(on_first, inner[near], inner[far])
        lead_ref[source, 0] = jnp.where(on_first, inner[early], inner[late])
        lead_ref[source, 1] = jnp.where(on_first, inner[3 - early], inner[3 - late])

    powers = [inner[3] * inner[1]]
    for _ in range(rounds):
        powers.append(powers[-1] * powers[-1])
    whole_decay = powers[-1] * decay

    def step_power(count, bits):
        result = one
        for bit in range(bits):
            result = jnp.where((count & (1 << bit)) != 0, result * powers[bit], result)
        return result

    for turn in range(rounds):
        reach = 1 << turn
        above = (team & reach) != 0
        offset = team & (reach - 1)
        mine = jnp.where(above, one, powers[turn])
        theirs = jnp.where(above, powers[turn], one)
        mix_ref[turn, 0, 0] = mine
        mix_ref[turn, 0, 1] = theirs
        mix_ref[turn, 1, 0] = theirs
        mix_ref[turn, 1, 1] = mine
        near_ref[turn, 0] = jnp.where(above, step_power(offset, turn), zero)
        near_ref[turn, 1] = jnp.where(above, zero, step_power(reach - 1 - offset, turn))
    closing = decay / (1.0 - whole_decay * whole_decay)
    to_first = closing * step_power(team, rounds)
    to_last = closing * step_power(teams - 1 - team, rounds)
    end_ref[0, 0] = to_first * whole_decay
    end_ref[0, 1] = -to_first
    end_ref[1, 0] = -to_last
    end_ref[1, 1] = to_last * whole_decay


def place_in_team():
    position = lax.axis_index("ax")
    core = lax.rem(position, jnp.int32(cores))
    chip = lax.div(position, jnp.int32(cores))
    return core, lax.rem(chip, jnp.int32(merge)), lax.div(chip, jnp.int32(merge))


def power(base, count):
    result = None
    while count:
        if count & 1:
            result = base if result is None else result * base
        base = base * base
        count >>= 1
    return result


def forward_kernel(even_ref, odd_ref, x_ref, out_ref):
    total, width = x_ref.shape
    blocks, size, _ = out_ref.shape
    half, quarter = total // 2, total // 4
    low, high = x_ref[:half], x_ref[half:]
    kept, turned = low + high, low - high
    parts = (
        (even_ref, 0, kept[:quarter] + kept[quarter:]),
        (even_ref, 1, kept[:quarter] - kept[quarter:]),
        (odd_ref, 0, turned),
    )
    at = 0
    for table_ref, which, folded in parts:
        rows = table_ref.shape[1] // blocks
        a, b, c = split3(folded)
        leading, rest = split2(table_ref[which])
        pair = jnp.concatenate([a, b], axis=1)
        first = mul(leading, pair) + mul(rest, pair)
        result = first[:, :width] + (first[:, width:] + mul(leading, c))
        out_ref[:, at : at + rows, :] = result.reshape(blocks, rows, width)
        at += rows


def backward_kernel(even_ref, odd_ref, x_ref, out_ref):
    blocks, size, width = x_ref.shape
    total = out_ref.shape[0]
    half, quarter = total // 2, total // 4
    sums = []
    at = 0
    for table_ref, which in ((even_ref, 0), (even_ref, 1), (odd_ref, 0)):
        rows = table_ref.shape[2] // blocks
        a, b = split2(x_ref[:, at : at + rows, :].reshape(rows * blocks, width))
        leading, rest = split2(table_ref[which])
        first = mul(leading, jnp.concatenate([a, b], axis=1))
        sums.append(first[:, :width] + (first[:, width:] + mul(rest, a)))
        at += rows
    fours, twos, odd = sums
    for which, even in enumerate((fours + twos, fours - twos)):
        part = odd[which * quarter : (which + 1) * quarter]
        out_ref[which * quarter : (which + 1) * quarter] = even + part
        out_ref[half + which * quarter : half + (which + 1) * quarter] = even - part


def modal_kernel(x_ref, basis_ref, weights_ref, decay_ref, f_ref, carry_ref):
    depth, size, _ = x_ref.shape
    weights = weights_ref[...]
    first = place_in_team()[1] * size
    tile = min(8, size)
    for group in range(0, size, tile):
        rows = jnp.swapaxes(x_ref[:, group : group + tile, :] * weights, 0, 1)
        results = []
        for inner in range(tile):
            values = jnp.concatenate(split3(rows[inner]), axis=0)
            basis = jnp.concatenate(split2(basis_ref[first + mode_offset(group + inner, size)]), axis=0)
            result = mul(twice(values, 1), basis)
            results.append(result[:depth] + (result[depth : 2 * depth] + result[2 * depth :]))
        f_ref[:, group : group + tile, :] = jnp.swapaxes(jnp.stack(results), 0, 1)
    decay = decay_ref[...]
    part = depth // merge
    ups = [f_ref[which * part] for which in range(merge)]
    downs = [f_ref[which * part + part - 1] for which in range(merge)]
    for step in range(1, part):
        for which in range(merge):
            ups[which] = ups[which] * decay + f_ref[which * part + step]
            downs[which] = downs[which] * decay + f_ref[which * part + part - 1 - step]
    for which in range(merge):
        carry_ref[which, 0] = ups[which]
        carry_ref[which, 1] = downs[which]


def solve_kernel(
    f_ref, basis_ref, decay_ref, gain_ref, link_ref, lead_ref, mix_ref, near_ref, end_ref, carry_ref, twin_ref, *refs
):
    *other_refs, out_ref, up_ref, down_ref = refs
    depth, size, _ = f_ref.shape
    part = depth // merge
    decay = decay_ref[...]
    first = place_in_team()[1] * size

    def within_team(target, end):
        terms = [
            link_ref[owner, target, source, end] * ref[source, end]
            for owner, ref in enumerate((carry_ref, twin_ref))
            for source in range(merge)
        ]
        return functools.reduce(jnp.add, terms)

    total = [within_team(merge, end) for end in range(2)]
    start = [jnp.zeros_like(decay)] * 2
    for turn, other_ref in enumerate(other_refs):
        other = [other_ref[0], other_ref[1]]
        start = [start[end] + near_ref[turn, end] * other[end] for end in range(2)]
        total = [mix_ref[turn, 0, end] * total[end] + mix_ref[turn, 1, end] * other[end] for end in range(2)]
    start = [start[end] + (end_ref[end, 0] * total[0] + end_ref[end, 1] * total[1]) for end in range(2)]
    ups, downs = (
        [within_team(which, end) + lead_ref[which, end] * start[end] for which in range(merge)] for end in range(2)
    )
    for step in range(part):
        for which in range(merge):
            low = which * part + step
            high = which * part + part - 1 - step
            ups[which] = ups[which] * decay
            up_ref[low] = ups[which]
            ups[which] = ups[which] + f_ref[low]
            downs[which] = downs[which] * decay + f_ref[high]
            down_ref[high] = downs[which]
    tile = min(8, size)
    for group in range(0, size, tile):
        part = slice(group, group + tile)
        rows = jnp.swapaxes((up_ref[:, part, :] + down_ref[:, part, :]) * gain_ref[part, :], 0, 1)
        results = []
        for inner in range(tile):
            values = jnp.concatenate(split2(rows[inner]), axis=0)
            basis = jnp.concatenate(split2(basis_ref[first + mode_offset(group + inner, size)]), axis=1)
            result = mul_t(twice(values, 1), basis)
            results.append(result[:depth] + result[depth:])
        out_ref[:, part, :] = jnp.swapaxes(jnp.stack(results), 0, 1)


def scatter_kernel(x_ref, out_ref, turned_ref, sems):
    cells, angles, _ = x_ref.shape
    chunks = sems.shape[0]
    rows = angles // chunks
    copies = []
    for chunk in range(chunks):
        swap_tiles(x_ref, turned_ref, range(chunk * rows, (chunk + 1) * rows, min(8, rows)), range(0, cells, min(8, cells)))
        part = pl.ds(chunk * rows, rows)
        copies.append(pltpu.make_async_copy(turned_ref.at[part], out_ref.at[part], sems.at[chunk]))
        copies[-1].start()
    for copy in copies:
        copy.wait()


def whole(memory_space=pltpu.VMEM):
    return pl.BlockSpec(memory_space=memory_space)


def in_vmem(value):
    return pltpu.with_memory_space_constraint(value, pltpu.VMEM)


def in_hbm(value):
    return pltpu.with_memory_space_constraint(value, pltpu.HBM)


def body(source, radial_basis, radial_weights, mode_shifts):
    planes = lax.axis_size("plane")
    blocks = lax.axis_size("ax")
    local_t, depth_cells, radius_count = source.shape
    total_t = local_t * planes
    size = local_t // merge
    span = depth_cells * merge
    teams = blocks // (merge * cores)
    tables = fourier_parts(total_t, planes, merge)
    forward_tables = [jnp.asarray(table) for table in tables]
    backward_tables = [jnp.asarray(table.transpose(0, 2, 1)) for table in tables]
    neighbours = [
        [
            plane * blocks + (team * merge + share) * cores + core
            for share in range(merge)
            for plane in range(planes)
        ]
        for team in range(teams)
        for core in range(cores)
    ]
    rounds = swaps(teams)

    turned, held_even, held_odd, decay, gain = pl.pallas_call(
        prepare_kernel,
        out_shape=(
            pltpu.VMEM((depth_cells, local_t, radius_count), f32),
            *(pltpu.VMEM(table.shape, f32) for table in forward_tables),
            pltpu.VMEM((size, radius_count), f32),
            pltpu.VMEM((size, radius_count), f32),
        ),
        in_specs=[whole(pltpu.HBM)] * 4,
        out_specs=(whole(),) * 5,
        scratch_shapes=[
            pltpu.VMEM(source.shape, f32),
            pltpu.VMEM((local_t + 8, radius_count), f32),
            pltpu.SemaphoreType.DMA((2,)),
            pltpu.SemaphoreType.DMA((3,)),
        ],
        name="cells_first",
        compiler_params=compact,
    )(in_hbm(source), in_hbm(mode_shifts), *map(in_hbm, forward_tables))
    piece = lax.all_to_all(turned, "plane", 0, 0, tiled=True)
    spectral = pl.pallas_call(
        forward_kernel,
        out_shape=pltpu.VMEM((planes * merge, size, radius_count), f32),
        in_specs=[whole()] * 3,
        out_specs=whole(),
        name="fourier_forward",
        compiler_params=compact,
    )(in_vmem(held_even), in_vmem(held_odd), in_vmem(piece.reshape(total_t, radius_count)))
    modal = lax.all_to_all(
        spectral, ("plane", "ax"), 0, 0, tiled=True, axis_index_groups=neighbours
    )
    spectra, carries = pl.pallas_call(
        modal_kernel,
        out_shape=(
            pltpu.VMEM((span, size, radius_count), f32),
            pltpu.VMEM((merge, 2, size, radius_count), f32),
        ),
        in_specs=[whole()] * 4,
        out_specs=(whole(), whole()),
        name="radial_forward",
        compiler_params=compact,
    )(in_vmem(modal), in_vmem(radial_basis), radial_weights.reshape(1, radius_count), in_vmem(decay))
    decay_then, carries = lax.optimization_barrier((decay, carries))
    link, lead, mix, near, ends = pl.pallas_call(
        functools.partial(factor_kernel, depth_cells),
        out_shape=(
            pltpu.VMEM((2, merge + 1, merge, 2, size, radius_count), f32),
            pltpu.VMEM((merge, 2, size, radius_count), f32),
            pltpu.VMEM((len(rounds), 2, 2, size, radius_count), f32),
            pltpu.VMEM((len(rounds), 2, size, radius_count), f32),
            pltpu.VMEM((2, 2, size, radius_count), f32),
        ),
        in_specs=[whole()],
        out_specs=(whole(),) * 5,
        name="carry_factors",
        compiler_params=compact,
        cost_estimate=pl.CostEstimate(flops=1_000_000, bytes_accessed=700_000, transcendentals=0),
    )(in_vmem(decay_then))
    twin = lax.ppermute(carries, "ax", [(index, index ^ 1) for index in range(blocks)])
    sent = (link[0, merge] * carries + link[1, merge] * twin).sum(axis=0)
    others = []
    for turn, partners in enumerate(rounds):
        if turn:
            sent = mix[turn - 1, 0] * sent + mix[turn - 1, 1] * others[-1]
        width = merge * cores
        pairs = [
            (team * width + member, partner * width + member)
            for team, partner in enumerate(partners)
            for member in range(width)
        ]
        others.append(lax.ppermute(sent, "ax", pairs))
    radial_field = pl.pallas_call(
        solve_kernel,
        out_shape=pltpu.VMEM((span, size, radius_count), f32),
        in_specs=[whole()] * (11 + len(rounds)),
        out_specs=whole(),
        scratch_shapes=[pltpu.VMEM((span, size, radius_count), f32)] * 2,
        name="solve_and_radial_back",
        compiler_params=compact,
    )(
        in_vmem(spectra),
        in_vmem(radial_basis),
        in_vmem(decay),
        in_vmem(gain),
        in_vmem(link),
        in_vmem(lead),
        in_vmem(mix),
        in_vmem(near),
        in_vmem(ends),
        in_vmem(carries),
        in_vmem(twin),
        *map(in_vmem, others),
    )
    collected = lax.all_to_all(
        radial_field, ("plane", "ax"), 0, 0, tiled=True, axis_index_groups=neighbours
    )
    spatial = pl.pallas_call(
        backward_kernel,
        out_shape=pltpu.VMEM((total_t, radius_count), f32),
        in_specs=[whole()] * 3,
        out_specs=whole(),
        name="fourier_backward",
        compiler_params=compact,
    )(*map(in_vmem, backward_tables), in_vmem(collected))
    pressure = lax.all_to_all(
        spatial.reshape(planes, local_t, radius_count), "plane", 0, 0, tiled=True
    )
    return pl.pallas_call(
        scatter_kernel,
        out_shape=jax.ShapeDtypeStruct(source.shape, f32),
        in_specs=[whole()],
        out_specs=whole(pltpu.HBM),
        scratch_shapes=[pltpu.VMEM(source.shape, f32), pltpu.SemaphoreType.DMA((4,))],
        name="angles_first",
        compiler_params=compact,
    )(in_vmem(pressure))


def solution(mesh):
    placed = (P("plane", "ax", None), P("plane", None, None), P(), P("plane", None))
    return jax.shard_map(
        body, mesh=mesh, in_specs=placed, out_specs=P("plane", "ax", None), check_vma=False
    )
```

```python
import functools
import math

import jax
import jax.numpy as jnp
import numpy as np
from jax import lax
from jax.experimental import pallas as pl
from jax.experimental.pallas import tpu as pltpu
from jax.sharding import PartitionSpec as P

axial_scale = 0.01
cores = 2
merge = 2
bf16 = jnp.bfloat16
f32 = jnp.float32
compact = pltpu.CompilerParams(vmem_limit_bytes=16 * 2**20)


def mode_offset(place, size):
    quarter = size // 4
    if place < quarter:
        return 4 * place
    if place < 2 * quarter:
        return 4 * (place - quarter) + 2
    return 2 * (place - 2 * quarter) + 1


def fourier_parts(total, planes, share):
    local = total // planes
    size = local // share
    bounds = (0, size // 4, size // 2, size)
    tables = []
    for which, columns in enumerate((total // 4, total // 4, total // 2)):
        offsets = np.array([mode_offset(place, size) for place in range(bounds[which], bounds[which + 1])])
        share_at, plane_at, offset = np.meshgrid(np.arange(share), np.arange(planes), offsets, indexing="ij")
        order = (plane_at * local + share_at * size + offset).reshape(-1)
        middle = total // 2
        harmonic = np.where(order <= middle, order, order - middle)
        radians = (harmonic[:, None] * np.arange(columns) % total) * (2.0 * math.pi / total)
        factor = np.where((order == 0) | (order == middle), math.sqrt(1.0 / total), math.sqrt(2.0 / total))
        waves = np.where((order <= middle)[:, None], np.cos(radians), np.sin(radians))
        tables.append((waves * factor[:, None]).astype(np.float32))
    return np.stack(tables[:2]), tables[2][None]


def split2(value):
    high = value.astype(bf16)
    return high, (value - high.astype(f32)).astype(bf16)


def split3(value):
    high = value.astype(bf16)
    rest = value - high.astype(f32)
    middle = rest.astype(bf16)
    return high, middle, (rest - middle.astype(f32)).astype(bf16)


def mul(left, right):
    return jnp.dot(left, right, preferred_element_type=f32)


def mul_t(left, right):
    return lax.dot_general(left, right, (((1,), (1,)), ((), ())), preferred_element_type=f32)


def twice(value, axis):
    return jnp.concatenate([value, value], axis=axis)


def swap_tiles(from_ref, to_ref, firsts, seconds):
    for first in firsts:
        for second in seconds:
            rows, columns = slice(first, first + firsts.step), slice(second, second + seconds.step)
            to_ref[rows, columns, :] = jnp.swapaxes(from_ref[columns, rows, :], 0, 1)


def swaps(teams):
    rounds = []
    reach = 1
    while reach < teams:
        if 2 * reach == teams and teams == 4:
            rounds.append([team ^ 3 for team in range(teams)])
        elif 2 * reach == teams and teams >= 8:
            wide = teams // 8
            far = (6, 7, 4, 5, 2, 3, 0, 1)
            rounds.append([far[team // wide] * wide + team % wide for team in range(teams)])
        else:
            rounds.append([team ^ reach for team in range(teams)])
        reach *= 2
    return rounds


def prepare_kernel(
    source_ref, shifts_ref, even_ref, odd_ref, out_ref, even_out_ref, odd_out_ref, decay_ref, gain_ref,
    held_ref, shift_ref, sems, extra_sems,
):
    cells, angles, _ = out_ref.shape
    size = decay_ref.shape[0]
    chunks = sems.shape[0]
    rows = angles // chunks
    shift_copy = pltpu.make_async_copy(
        shifts_ref, shift_ref.at[pl.ds(0, shifts_ref.shape[0])], extra_sems.at[0]
    )
    table_copies = [
        pltpu.make_async_copy(even_ref, even_out_ref, extra_sems.at[1]),
        pltpu.make_async_copy(odd_ref, odd_out_ref, extra_sems.at[2]),
    ]
    copies = [
        pltpu.make_async_copy(
            source_ref.at[pl.ds(chunk * rows, rows)], held_ref.at[pl.ds(chunk * rows, rows)], sems.at[chunk]
        )
        for chunk in range(chunks)
    ]
    shift_copy.start()
    for copy in copies:
        copy.start()
    for copy in table_copies:
        copy.start()

    first = place_in_team()[1] * size
    shift_copy.wait()
    shifts = jnp.concatenate(
        [
            shift_ref[pl.ds(first, size // 4, stride=4), :],
            shift_ref[pl.ds(first + 2, size // 4, stride=4), :],
            shift_ref[pl.ds(first + 1, size // 2, stride=2), :],
        ],
        axis=0,
    )
    rise = 0.5 * jnp.sqrt((2.0 + shifts) - 2.0)
    cosh_half = jnp.sqrt(1.0 + rise * rise)
    root = cosh_half - rise
    decay = root * root
    decay_ref[...] = decay
    gain_ref[...] = axial_scale / (4.0 * rise * cosh_half)
    for chunk, copy in enumerate(copies):
        copy.wait()
        swap_tiles(held_ref, out_ref, range(0, cells, min(8, cells)), range(chunk * rows, (chunk + 1) * rows, min(8, rows)))
    for copy in table_copies:
        copy.wait()


def factor_kernel(cells, decay_ref, link_ref, lead_ref, mix_ref, near_ref, end_ref):
    rounds = near_ref.shape[0]
    teams = 2**rounds
    core, _, team = place_in_team()
    decay = decay_ref[...]
    one = jnp.ones_like(decay)
    zero = jnp.zeros_like(decay)

    inner = [one, power(decay, cells)]
    for _ in range(2):
        inner.append(inner[-1] * inner[1])
    on_first = core == 0

    def apart(distance):
        below = inner[-distance - 1] if distance < 0 else zero
        above = inner[distance - 1] if distance > 0 else zero
        return below, above

    for source in range(merge):
        for target in range(merge):
            gap = 2 * (source - target)
            for end in range(2):
                link_ref[0, target, source, end] = apart(gap)[end]
                link_ref[1, target, source, end] = jnp.where(
                    on_first, apart(gap + 1)[end], apart(gap - 1)[end]
                )
        early, late = 2 * source, 2 * source + 1
        for owner in range(2):
            near, far = (early, late) if owner == 0 else (late, early)
            link_ref[owner, merge, source, 0] = jnp.where(on_first, inner[3 - near], inner[3 - far])
            link_ref[owner, merge, source, 1] = jnp.where(on_first, inner[near], inner[far])
        lead_ref[source, 0] = jnp.where(on_first, inner[early], inner[late])
        lead_ref[source, 1] = jnp.where(on_first, inner[3 - early], inner[3 - late])

    powers = [inner[3] * inner[1]]
    for _ in range(rounds):
        powers.append(powers[-1] * powers[-1])
    whole_decay = powers[-1] * decay

    def step_power(count, bits):
        result = one
        for bit in range(bits):
            result = jnp.where((count & (1 << bit)) != 0, result * powers[bit], result)
        return result

    for turn in range(rounds):
        reach = 1 << turn
        above = (team & reach) != 0
        offset = team & (reach - 1)
        mine = jnp.where(above, one, powers[turn])
        theirs = jnp.where(above, powers[turn], one)
        mix_ref[turn, 0, 0] = mine
        mix_ref[turn, 0, 1] = theirs
        mix_ref[turn, 1, 0] = theirs
        mix_ref[turn, 1, 1] = mine
        near_ref[turn, 0] = jnp.where(above, step_power(offset, turn), zero)
        near_ref[turn, 1] = jnp.where(above, zero, step_power(reach - 1 - offset, turn))
    closing = decay / (1.0 - whole_decay * whole_decay)
    to_first = closing * step_power(team, rounds)
    to_last = closing * step_power(teams - 1 - team, rounds)
    end_ref[0, 0] = to_first * whole_decay
    end_ref[0, 1] = -to_first
    end_ref[1, 0] = -to_last
    end_ref[1, 1] = to_last * whole_decay


def place_in_team():
    position = lax.axis_index("ax")
    core = lax.rem(position, jnp.int32(cores))
    chip = lax.div(position, jnp.int32(cores))
    return core, lax.rem(chip, jnp.int32(merge)), lax.div(chip, jnp.int32(merge))


def power(base, count):
    result = None
    while count:
        if count & 1:
            result = base if result is None else result * base
        base = base * base
        count >>= 1
    return result


def forward_kernel(even_ref, odd_ref, x_ref, out_ref):
    total, width = x_ref.shape
    blocks, size, _ = out_ref.shape
    half, quarter = total // 2, total // 4
    low, high = x_ref[:half], x_ref[half:]
    kept, turned = low + high, low - high
    parts = (
        (even_ref, 0, kept[:quarter] + kept[quarter:]),
        (even_ref, 1, kept[:quarter] - kept[quarter:]),
        (odd_ref, 0, turned),
    )
    at = 0
    for table_ref, which, folded in parts:
        rows = table_ref.shape[1] // blocks
        a, b, c = split3(folded)
        leading, rest = split2(table_ref[which])
        pair = jnp.concatenate([a, b], axis=1)
        first = mul(leading, pair) + mul(rest, pair)
        result = first[:, :width] + (first[:, width:] + mul(leading, c))
        out_ref[:, at : at + rows, :] = result.reshape(blocks, rows, width)
        at += rows


def backward_kernel(even_ref, odd_ref, x_ref, out_ref):
    blocks, size, width = x_ref.shape
    total = out_ref.shape[0]
    half, quarter = total // 2, total // 4
    sums = []
    at = 0
    for table_ref, which in ((even_ref, 0), (even_ref, 1), (odd_ref, 0)):
        rows = table_ref.shape[2] // blocks
        a, b = split2(x_ref[:, at : at + rows, :].reshape(rows * blocks, width))
        leading, rest = split2(table_ref[which])
        first = mul(leading, jnp.concatenate([a, b], axis=1))
        sums.append(first[:, :width] + (first[:, width:] + mul(rest, a)))
        at += rows
    fours, twos, odd = sums
    for which, even in enumerate((fours + twos, fours - twos)):
        part = odd[which * quarter : (which + 1) * quarter]
        out_ref[which * quarter : (which + 1) * quarter] = even + part
        out_ref[half + which * quarter : half + (which + 1) * quarter] = even - part


def modal_kernel(x_ref, basis_ref, weights_ref, decay_ref, f_ref, carry_ref):
    depth, size, _ = x_ref.shape
    weights = weights_ref[...]
    first = place_in_team()[1] * size
    tile = min(8, size)
    for group in range(0, size, tile):
        rows = jnp.swapaxes(x_ref[:, group : group + tile, :] * weights, 0, 1)
        results = []
        width = rows.shape[2]
        for inner in range(0, tile, 2):
            values = jnp.concatenate(split3(rows[inner]) + split3(rows[inner + 1]), axis=0)
            pair = [
                jnp.concatenate(split2(basis_ref[first + mode_offset(group + which, size)]), axis=0)
                for which in (inner, inner + 1)
            ]
            both = mul(twice(values, 1), jnp.concatenate(pair, axis=1))
            for half in (both[: 3 * depth, :width], both[3 * depth :, width:]):
                results.append(half[:depth] + (half[depth : 2 * depth] + half[2 * depth :]))
        f_ref[:, group : group + tile, :] = jnp.swapaxes(jnp.stack(results), 0, 1)
    decay = decay_ref[...]
    part = depth // merge
    ups = [f_ref[which * part] for which in range(merge)]
    downs = [f_ref[which * part + part - 1] for which in range(merge)]
    for step in range(1, part):
        for which in range(merge):
            ups[which] = ups[which] * decay + f_ref[which * part + step]
            downs[which] = downs[which] * decay + f_ref[which * part + part - 1 - step]
    for which in range(merge):
        carry_ref[which, 0] = ups[which]
        carry_ref[which, 1] = downs[which]


def solve_kernel(
    f_ref, basis_ref, decay_ref, gain_ref, link_ref, lead_ref, mix_ref, near_ref, end_ref, carry_ref, twin_ref, *refs
):
    *other_refs, out_ref, up_ref, down_ref = refs
    depth, size, _ = f_ref.shape
    part = depth // merge
    decay = decay_ref[...]
    first = place_in_team()[1] * size

    def within_team(target, end):
        terms = [
            link_ref[owner, target, source, end] * ref[source, end]
            for owner, ref in enumerate((carry_ref, twin_ref))
            for source in range(merge)
        ]
        return functools.reduce(jnp.add, terms)

    total = [within_team(merge, end) for end in range(2)]
    start = [jnp.zeros_like(decay)] * 2
    for turn, other_ref in enumerate(other_refs):
        other = [other_ref[0], other_ref[1]]
        start = [start[end] + near_ref[turn, end] * other[end] for end in range(2)]
        total = [mix_ref[turn, 0, end] * total[end] + mix_ref[turn, 1, end] * other[end] for end in range(2)]
    start = [start[end] + (end_ref[end, 0] * total[0] + end_ref[end, 1] * total[1]) for end in range(2)]
    ups, downs = (
        [within_team(which, end) + lead_ref[which, end] * start[end] for which in range(merge)] for end in range(2)
    )
    for step in range(part):
        for which in range(merge):
            low = which * part + step
            high = which * part + part - 1 - step
            ups[which] = ups[which] * decay
            up_ref[low] = ups[which]
            ups[which] = ups[which] + f_ref[low]
            downs[which] = downs[which] * decay + f_ref[high]
            down_ref[high] = downs[which]
    tile = min(8, size)
    for group in range(0, size, tile):
        part = slice(group, group + tile)
        rows = jnp.swapaxes((up_ref[:, part, :] + down_ref[:, part, :]) * gain_ref[part, :], 0, 1)
        results = []
        width = rows.shape[2]
        for inner in range(0, tile, 2):
            values = jnp.concatenate(split2(rows[inner]) + split2(rows[inner + 1]), axis=0)
            pair = [
                jnp.concatenate(split2(basis_ref[first + mode_offset(group + which, size)]), axis=1)
                for which in (inner, inner + 1)
            ]
            both = mul_t(twice(values, 1), jnp.concatenate(pair, axis=0))
            for half in (both[: 2 * depth, :width], both[2 * depth :, width:]):
                results.append(half[:depth] + half[depth:])
        out_ref[:, part, :] = jnp.swapaxes(jnp.stack(results), 0, 1)


def scatter_kernel(x_ref, out_ref, turned_ref, sems):
    cells, angles, _ = x_ref.shape
    chunks = sems.shape[0]
    rows = angles // chunks
    copies = []
    for chunk in range(chunks):
        swap_tiles(x_ref, turned_ref, range(chunk * rows, (chunk + 1) * rows, min(8, rows)), range(0, cells, min(8, cells)))
        part = pl.ds(chunk * rows, rows)
        copies.append(pltpu.make_async_copy(turned_ref.at[part], out_ref.at[part], sems.at[chunk]))
        copies[-1].start()
    for copy in copies:
        copy.wait()


def whole(memory_space=pltpu.VMEM):
    return pl.BlockSpec(memory_space=memory_space)


def in_vmem(value):
    return pltpu.with_memory_space_constraint(value, pltpu.VMEM)


def in_hbm(value):
    return pltpu.with_memory_space_constraint(value, pltpu.HBM)


def body(source, radial_basis, radial_weights, mode_shifts):
    planes = lax.axis_size("plane")
    blocks = lax.axis_size("ax")
    local_t, depth_cells, radius_count = source.shape
    total_t = local_t * planes
    size = local_t // merge
    span = depth_cells * merge
    teams = blocks // (merge * cores)
    tables = fourier_parts(total_t, planes, merge)
    forward_tables = [jnp.asarray(table) for table in tables]
    backward_tables = [jnp.asarray(table.transpose(0, 2, 1)) for table in tables]
    neighbours = [
        [
            plane * blocks + (team * merge + share) * cores + core
            for share in range(merge)
            for plane in range(planes)
        ]
        for team in range(teams)
        for core in range(cores)
    ]
    rounds = swaps(teams)

    turned, held_even, held_odd, decay, gain = pl.pallas_call(
        prepare_kernel,
        out_shape=(
            pltpu.VMEM((depth_cells, local_t, radius_count), f32),
            *(pltpu.VMEM(table.shape, f32) for table in forward_tables),
            pltpu.VMEM((size, radius_count), f32),
            pltpu.VMEM((size, radius_count), f32),
        ),
        in_specs=[whole(pltpu.HBM)] * 4,
        out_specs=(whole(),) * 5,
        scratch_shapes=[
            pltpu.VMEM(source.shape, f32),
            pltpu.VMEM((local_t + 8, radius_count), f32),
            pltpu.SemaphoreType.DMA((2,)),
            pltpu.SemaphoreType.DMA((3,)),
        ],
        name="cells_first",
        compiler_params=compact,
    )(in_hbm(source), in_hbm(mode_shifts), *map(in_hbm, forward_tables))
    piece = lax.all_to_all(turned, "plane", 0, 0, tiled=True)
    spectral = pl.pallas_call(
        forward_kernel,
        out_shape=pltpu.VMEM((planes * merge, size, radius_count), f32),
        in_specs=[whole()] * 3,
        out_specs=whole(),
        name="fourier_forward",
        compiler_params=compact,
    )(in_vmem(held_even), in_vmem(held_odd), in_vmem(piece.reshape(total_t, radius_count)))
    modal = lax.all_to_all(
        spectral, ("plane", "ax"), 0, 0, tiled=True, axis_index_groups=neighbours
    )
    spectra, carries = pl.pallas_call(
        modal_kernel,
        out_shape=(
            pltpu.VMEM((span, size, radius_count), f32),
            pltpu.VMEM((merge, 2, size, radius_count), f32),
        ),
        in_specs=[whole()] * 4,
        out_specs=(whole(), whole()),
        name="radial_forward",
        compiler_params=compact,
    )(in_vmem(modal), in_vmem(radial_basis), radial_weights.reshape(1, radius_count), in_vmem(decay))
    decay_then, carries = lax.optimization_barrier((decay, carries))
    link, lead, mix, near, ends = pl.pallas_call(
        functools.partial(factor_kernel, depth_cells),
        out_shape=(
            pltpu.VMEM((2, merge + 1, merge, 2, size, radius_count), f32),
            pltpu.VMEM((merge, 2, size, radius_count), f32),
            pltpu.VMEM((len(rounds), 2, 2, size, radius_count), f32),
            pltpu.VMEM((len(rounds), 2, size, radius_count), f32),
            pltpu.VMEM((2, 2, size, radius_count), f32),
        ),
        in_specs=[whole()],
        out_specs=(whole(),) * 5,
        name="carry_factors",
        compiler_params=compact,
        cost_estimate=pl.CostEstimate(flops=1_000_000, bytes_accessed=700_000, transcendentals=0),
    )(in_vmem(decay_then))
    twin = lax.ppermute(carries, "ax", [(index, index ^ 1) for index in range(blocks)])
    sent = (link[0, merge] * carries + link[1, merge] * twin).sum(axis=0)
    others = []
    for turn, partners in enumerate(rounds):
        if turn:
            sent = mix[turn - 1, 0] * sent + mix[turn - 1, 1] * others[-1]
        width = merge * cores
        pairs = [
            (team * width + member, partner * width + member)
            for team, partner in enumerate(partners)
            for member in range(width)
        ]
        others.append(lax.ppermute(sent, "ax", pairs))
    radial_field = pl.pallas_call(
        solve_kernel,
        out_shape=pltpu.VMEM((span, size, radius_count), f32),
        in_specs=[whole()] * (11 + len(rounds)),
        out_specs=whole(),
        scratch_shapes=[pltpu.VMEM((span, size, radius_count), f32)] * 2,
        name="solve_and_radial_back",
        compiler_params=compact,
    )(
        in_vmem(spectra),
        in_vmem(radial_basis),
        in_vmem(decay),
        in_vmem(gain),
        in_vmem(link),
        in_vmem(lead),
        in_vmem(mix),
        in_vmem(near),
        in_vmem(ends),
        in_vmem(carries),
        in_vmem(twin),
        *map(in_vmem, others),
    )
    collected = lax.all_to_all(
        radial_field, ("plane", "ax"), 0, 0, tiled=True, axis_index_groups=neighbours
    )
    spatial = pl.pallas_call(
        backward_kernel,
        out_shape=pltpu.VMEM((total_t, radius_count), f32),
        in_specs=[whole()] * 3,
        out_specs=whole(),
        name="fourier_backward",
        compiler_params=compact,
    )(*map(in_vmem, backward_tables), in_vmem(collected))
    pressure = lax.all_to_all(
        spatial.reshape(planes, local_t, radius_count), "plane", 0, 0, tiled=True
    )
    return pl.pallas_call(
        scatter_kernel,
        out_shape=jax.ShapeDtypeStruct(source.shape, f32),
        in_specs=[whole()],
        out_specs=whole(pltpu.HBM),
        scratch_shapes=[pltpu.VMEM(source.shape, f32), pltpu.SemaphoreType.DMA((4,))],
        name="angles_first",
        compiler_params=compact,
    )(in_vmem(pressure))


def solution(mesh):
    placed = (P("plane", "ax", None), P("plane", None, None), P(), P("plane", None))
    return jax.shard_map(
        body, mesh=mesh, in_specs=placed, out_specs=P("plane", "ax", None), check_vma=False
    )
```
